512 devices in a mesh: wide: 64 (over z, x, core), narrow: 8 (over y).
Axes of the slice: x: 4, y: 8, z: 8, core: 2. Of those that a mesh axis runs over, the one named last changes fastest.
Arguments:
- fields: float32 [2, 64, 2048, 1024], P(None, 'narrow', 'wide'), may hold values from -6 to 6
- field_bins: int32 [2, 64, 2048, 1024], P(None, 'narrow', 'wide'), may hold values from 0 to 255
- colour_table: bfloat16 [2, 3, 256], replicated, may hold values from 0.049804688 to 1
- opacity_table: bfloat16 [2, 256], replicated, may hold values from 0.00049972534 to 0.0099487305
- view_dir: int32 [2048], P('wide'), may hold values from 0 to 1
Outputs:
- frame: float32 [4, 2048, 1024], P(None, None, 'narrow')
The draws below stay inside these ranges and needn't reach their ends.
Inputs may be any that keep to these rules, and one draw needn't show every extreme that they name: `view_dir`: 0: the column's rays travel toward increasing depth index; 1: toward decreasing depth index.
All inputs are finite; a program needn't handle non-finite values.
Results may differ from the reference program's by a relative error of at most 0.0003.
Values sent between devices are 32-bit elements; how exact they have to be, the bound alone decides.
No kernel may reach another device: no remote copies, remote signals or barrier semaphores. Data moves between devices by JAX's collectives and lax.ppermute only.
A program may use at most 64 MiB of HBM per device.

```python
import math
import jax
import jax.numpy as jnp
from jax import lax

BINS = 256
NX = 2048
BY = 1024
NZ = 64


def set_ends(values, stream_key, smallest, high):
    place = [jax.random.randint(jax.random.fold_in(stream_key, axis), (), 0, length) for axis, length in enumerate(values.shape)]
    longest = values.shape.index(max(values.shape))
    beside = place[:longest] + [(place[longest] + 1) % values.shape[longest]] + place[longest + 1:]
    return values.at[tuple(place)].set(smallest).at[tuple(beside)].set(high)


def levels(key, extent, shards, least, largest):
    factor_of, own = 1.0, jax.random.fold_in(key, 6)
    for position, blocks in shards:
        draws = jnp.exp(jax.random.uniform(jax.random.fold_in(own, position), (blocks,), jnp.float32, least / len(shards), largest / len(shards)))
        factor_of = factor_of * jnp.repeat(draws, extent[position] // blocks).reshape([-1 if axis == position else 1 for axis in range(len(extent))])
    return factor_of


def centred(key, dims, deviation, bound, cuts=(), held_as=jnp.bfloat16):
    level = levels(key, dims, cuts, -0.22, 0.18) if cuts else 1.0
    values = jax.random.normal(key, dims, jnp.float32) * deviation * level
    return jnp.minimum(jnp.maximum(values, -bound), bound).astype(held_as)


def setup_inputs(seed: int = 0) -> dict:
    splits = jax.random.split(jax.random.key(seed), 6)
    return {
        "fields": centred(splits[0], (2, NZ, NX, BY), 1.0, 6.0, ((1, 8), (2, 64)), jnp.float32),
        "field_bins": set_ends(jax.random.randint(splits[1], (2, NZ, NX, BY), 0, BINS), jax.random.fold_in(splits[1], 1), 0, BINS - 1).astype(jnp.int32),
        "colour_table": jnp.clip(jax.random.uniform(splits[2], (2, 3, BINS), jnp.float32, 0.049804688, 1.0), 0.049804688, 1.0).astype(jnp.bfloat16),
        "opacity_table": jnp.clip(jnp.exp(jax.random.uniform(splits[3], (2, BINS), jnp.float32, math.log(0.00049972534), math.log(0.0099487305))), 0.00049972534, 0.0099487305).astype(jnp.bfloat16),
        "view_dir": set_ends(jax.random.randint(splits[4], (NX,), 0, 2), jax.random.fold_in(splits[4], 1), 0, 1).astype(jnp.int32),
    }


def gradient_terms(padded):
    grad_depth = 0.5 * (padded[:, 2:, 1:-1, 1:-1] - padded[:, :-2, 1:-1, 1:-1])
    grad_column = 0.5 * (padded[:, 1:-1, 2:, 1:-1] - padded[:, 1:-1, :-2, 1:-1])
    grad_row = 0.5 * (padded[:, 1:-1, 1:-1, 2:] - padded[:, 1:-1, 1:-1, :-2])
    square = grad_depth * grad_depth + grad_column * grad_column + grad_row * grad_row
    shading = 0.3 + 0.7 * jnp.abs(grad_depth) / jnp.sqrt(square + 1.0)
    return (shading, 0.25 + jnp.sqrt(square))

def make_sample(shading, opacity_gain, looked_up):
    opacity = looked_up[:, 3] * opacity_gain
    colour = opacity[0] * shading[0] * looked_up[0, :3] + opacity[1] * shading[1] * looked_up[1, :3]
    combined = 1.0 - (1.0 - opacity[0]) * (1.0 - opacity[1])
    return jnp.concatenate([colour, combined[None]], axis=0)

def blend_over(nearer, behind):
    return nearer + (1.0 - nearer[3:4]) * behind

def reference(fields, field_bins, colour_table, opacity_table, view_dir):
    backward = (view_dir == 1)[None, None, :, None]
    padded = jnp.pad(fields, ((0, 0), (1, 1), (1, 1), (1, 1)))
    depth_count = fields.shape[1]

    def terms_at(depth_index):
        depth_slab = lax.dynamic_slice_in_dim(padded, depth_index, 3, axis=1)
        shading, opacity_gain = gradient_terms(depth_slab)
        bins_now = lax.dynamic_slice_in_dim(field_bins, depth_index, 1, axis=1)
        return (shading, opacity_gain, bins_now)

    def march_step(running, order_step):
        shade_fwd, gain_fwd, bins_fwd = terms_at(order_step)
        shade_bwd, gain_bwd, bins_bwd = terms_at(depth_count - 1 - order_step)
        shading = jnp.where(backward, shade_bwd, shade_fwd)[:, 0]
        opacity_gain = jnp.where(backward, gain_bwd, gain_fwd)[:, 0]
        bins_now = jnp.where(backward, bins_bwd, bins_fwd)[:, 0]
        looked_up = jnp.stack([jnp.concatenate([colour_table[field_no][:, bins_now[field_no]], opacity_table[field_no][bins_now[field_no]][None]], axis=0) for field_no in range(2)]).astype(jnp.float32)
        return (blend_over(running, make_sample(shading, opacity_gain, looked_up)), None)
    start = jnp.zeros((4, fields.shape[2], fields.shape[3]), jnp.float32)
    frame, unused = lax.scan(march_step, start, jnp.arange(depth_count, dtype=jnp.int32))
    return frame
```

```python
import jax
import jax.numpy as jnp
from jax import lax
from jax.experimental import pallas as pl
from jax.experimental.pallas import tpu as pltpu
from jax.sharding import Mesh, PartitionSpec as P

LOOK = lax.GatherDimensionNumbers(offset_dims=(), collapsed_slice_dims=(1,), start_index_map=(1,), operand_batching_dims=(0,), start_indices_batching_dims=(0,))

def pick(table, lanes):
    return lax.gather(table, lanes[..., None], LOOK, (1, 1), mode=lax.GatherScatterMode.PROMISE_IN_BOUNDS)

def packed_tables(colour, opacity):
    words = []
    for f in range(2):
        c = [(colour[f, k:k+1, :].astype(jnp.float32) * 4096.0).astype(jnp.int32) for k in range(3)]
        o = (opacity[f:f+1, :].astype(jnp.float32) * 262144.0).astype(jnp.int32)
        w0 = c[0] + c[1] * 8192
        w1 = c[2] + o * 8192
        words.append([[jnp.broadcast_to(w[:, h*128:(h+1)*128], (8, 128)) for h in range(2)] for w in (w0, w1)])
    return words

def brick_kernel(fields, zlo, zhi, xlo, xhi, bins, ctab, otab, back, out, ext, tab):
    depth, cols, rows = fields.shape[1:]
    for f in range(2):
        ext[f, 0, 8:8+cols, 128:128+rows] = zlo[f, 0]
        ext[f, depth+1, 8:8+cols, 128:128+rows] = zhi[f, 0]
        for d in range(depth):
            ext[f, d+1, 8:8+cols, 128:128+rows] = fields[f, d]
            ext[f, d+1, 7:8, 128:128+rows] = xlo[f, d]
            ext[f, d+1, 8+cols:9+cols, 128:128+rows] = xhi[f, d]
            zero = jnp.zeros((cols, 128), jnp.float32)
            ext[f, d+1, 8:8+cols, 0:128] = zero
            ext[f, d+1, 8:8+cols, 128+rows:256+rows] = zero
    words = packed_tables(ctab[...], otab[...])
    for f in range(2):
        for w in range(2):
            for h in range(2):
                tab[f, w, h] = words[f][w][h]
    sub = lax.broadcasted_iota(jnp.int32, (8, 128), 0)
    lane = lax.broadcasted_iota(jnp.int32, (8, 128), 1)
    last_sub, first_sub = sub == 7, sub == 0
    last_lane, first_lane = lane == 127, lane == 0

    def tile(step, carry):
        g = step // (rows // 128)
        b = step % (rows // 128)
        c0 = pl.multiple_of(g * 8, 8)
        r0 = pl.multiple_of(b * 128, 128)
        backward = back[pl.ds(c0, 8), :] == 1
        acc = [None] * 3
        through = None
        for d in range(depth):
            part = [None] * 3
            clear = None
            for f in range(2):
                def at(dd, dc, dr):
                    return ext[f, d + 1 + dd, pl.ds(c0 + 8 + dc, 8), pl.ds(r0 + 128 + dr, 128)]
                here = at(0, 0, 0)
                dz = at(1, 0, 0) - at(-1, 0, 0)
                dx = pltpu.roll(jnp.where(first_sub, at(0, 8, 0), here), 7, 0) - pltpu.roll(jnp.where(last_sub, at(0, -8, 0), here), 1, 0)
                dy = pltpu.roll(jnp.where(first_lane, at(0, 0, 128), here), 127, 1) - pltpu.roll(jnp.where(last_lane, at(0, 0, -128), here), 1, 1)
                total = dz * dz + dx * dx + dy * dy
                shade = 0.3 + (0.35 * jnp.abs(dz)) * lax.rsqrt(0.25 * total + 1.0)
                scale = 2.0 ** -18
                gain = 0.25 * scale + (0.5 * scale) * (total * lax.rsqrt(jnp.maximum(total, 1e-30)))
                idx = bins[f, d, pl.ds(c0, 8), pl.ds(r0, 128)]
                low = idx & 127
                upper = idx > 127
                w = [jnp.where(upper, pick(tab[f, k, 1], low), pick(tab[f, k, 0], low)) for k in range(2)]
                look = [(w[0] & 8191).astype(jnp.float32), (w[0] >> 13).astype(jnp.float32), (w[1] & 8191).astype(jnp.float32)]
                alpha = (w[1] >> 13).astype(jnp.float32) * gain
                lit = alpha * shade
                for k in range(3):
                    term = lit * look[k]
                    part[k] = term if part[k] is None else part[k] + term
                clear = (1.0 - alpha) if clear is None else clear * (1.0 - alpha)
            if d == 0:
                acc = part
                through = clear
            else:
                keep = jnp.where(backward, clear, 1.0)
                weight = jnp.where(backward, 1.0, through)
                acc = [a * keep + weight * p for a, p in zip(acc, part)]
                through = through * clear
        for k in range(3):
            out[b, k, pl.ds(c0, 8), :] = acc[k] * (1.0 / 4096.0)
        out[b, 3, pl.ds(c0, 8), :] = 1.0 - through
        return carry
    lax.fori_loop(0, (cols // 8) * (rows // 128), tile, 0)

def brick(fields, zlo, zhi, xlo, xhi, bins, ctab, otab, back):
    _, depth, cols, rows = fields.shape
    return pl.pallas_call(
        brick_kernel,
        out_shape=jax.ShapeDtypeStruct((rows // 128, 4, cols, 128), jnp.float32),
        in_specs=[pl.BlockSpec(memory_space=pltpu.VMEM)] * 9,
        out_specs=pl.BlockSpec(memory_space=pltpu.VMEM),
        scratch_shapes=[pltpu.VMEM((2, depth + 2, cols + 16, rows + 256), jnp.float32), pltpu.VMEM((2, 2, 2, 8, 128), jnp.int32)],
        compiler_params=pltpu.CompilerParams(vmem_limit_bytes=40 * 2**20),
        name="brick",
    )(fields, zlo, zhi, xlo, xhi, bins, ctab, otab, back)


def join_kernel(parts, back, out):
    depth = parts.shape[0]
    for group in range(parts.shape[2] // 8):
        cols = pl.ds(group * 8, 8)
        backward = back[cols, :] == 1
        acc = [parts[0, k, cols, :] for k in range(3)]
        through = 1.0 - parts[0, 3, cols, :]
        for d in range(1, depth):
            clear = 1.0 - parts[d, 3, cols, :]
            keep = jnp.where(backward, clear, 1.0)
            weight = jnp.where(backward, 1.0, through)
            acc = [a * keep + weight * parts[d, k, cols, :] for k, a in enumerate(acc)]
            through = through * clear
        for k in range(3):
            out[k, cols, :] = acc[k]
        out[3, cols, :] = 1.0 - through


def join(parts, back):
    return pl.pallas_call(
        join_kernel,
        out_shape=jax.ShapeDtypeStruct(parts.shape[1:], jnp.float32),
        in_specs=[pl.BlockSpec(memory_space=pltpu.VMEM)] * 2,
        out_specs=pl.BlockSpec(memory_space=pltpu.VMEM),
        name="join",
    )(parts, back)


def place_kernel(spots, *refs):
    pieces, out, sem = refs[:-2], refs[-2], refs[-1]
    x_count = len(pieces) // 2
    copies = []
    for n, piece in enumerate(pieces):
        for z in range(piece.shape[0]):
            spot = out.at[:, z, spots[n % x_count], spots[x_count + n // x_count]]
            copies.append(pltpu.make_async_copy(piece.at[z], spot, sem))
    for copy in copies:
        copy.start()
    for copy in copies:
        copy.wait()


def place(pieces, others, spots):
    x_count = len(pieces)
    z_count, channels, cols, rows = pieces[0].shape
    frame = pl.pallas_call(
        place_kernel,
        out_shape=jax.ShapeDtypeStruct((channels, z_count, x_count, 2, cols, rows), jnp.float32),
        in_specs=[pl.BlockSpec(memory_space=pltpu.SMEM)] + [pl.BlockSpec(memory_space=pl.ANY)] * (2 * x_count),
        out_specs=pl.BlockSpec(memory_space=pl.ANY),
        scratch_shapes=[pltpu.SemaphoreType.DMA],
        name="place",
    )(spots, *pieces, *others)
    return frame.reshape(channels, z_count * x_count * 2 * cols, rows)


def shifted(value, axis, step, wrap=True):
    count = lax.axis_size(axis)
    route = [(i, (i + step) % count) for i in range(count) if wrap or 0 <= i + step < count]
    return lax.ppermute(value, axis, route)


def neighbour(value, step):
    axes = ("z", "x", "c")
    count = 1
    for axis in axes:
        count *= lax.axis_size(axis)
    return lax.ppermute(value, axes, [(i, i + step) for i in range(count) if 0 <= i + step < count])


def on_device(fields, field_bins, colour_table, opacity_table, view_dir):
    depth, cols = fields.shape[1:3]
    zlo = shifted(fields[:, depth - 1 :], "y", 1, wrap=False)
    zhi = shifted(fields[:, :1], "y", -1, wrap=False)
    xlo = neighbour(fields[:, :, cols - 1 :], 1)
    xhi = neighbour(fields[:, :, :1], -1)
    back = jnp.broadcast_to(view_dir[:, None], (cols, 128))
    partial = brick(fields, zlo, zhi, xlo, xhi, field_bins, colour_table, opacity_table, back)
    partial = lax.all_to_all(partial, "y", 0, 0)
    finished = join(partial, back)
    column = lax.all_gather(finished, "z")
    x_count = lax.axis_size("x")
    steps = [0, 1, x_count - 1] + list(range(2, x_count - 1))
    pieces = [column] + [shifted(column, "x", -step) for step in steps[1:]]
    others = [lax.ppermute(piece, "c", [(0, 1), (1, 0)]) for piece in pieces]
    x, c = lax.axis_index("x"), lax.axis_index("c")
    spots = jnp.stack([(x + step) % x_count for step in steps] + [c, 1 - c])
    return place(pieces, others, spots)


def solution(mesh):
    z_count, x_count, c_count = 8, 4, 2
    grid = Mesh(mesh.devices.reshape(z_count, x_count, c_count, -1), ("z", "x", "c", "y"))
    wide = ("z", "x", "c")
    in_specs = (
        P(None, "y", wide, None),
        P(None, "y", wide, None),
        P(),
        P(),
        P(wide),
    )
    return jax.shard_map(on_device, mesh=grid, in_specs=in_specs, out_specs=P(None, None, "y"), check_vma=False)
```

```python
import jax
import jax.numpy as jnp
from jax import lax
from jax.experimental import pallas as pl
from jax.experimental.pallas import tpu as pltpu
from jax.sharding import Mesh, PartitionSpec as P

LANES = 128
SUBS = 8
COLOUR_UNIT = 2.0**-12
OPACITY_UNIT = 2.0**-18
FIELD = 1 << 13

LOOKUP = lax.GatherDimensionNumbers(
    offset_dims=(),
    collapsed_slice_dims=(1,),
    start_index_map=(1,),
    operand_batching_dims=(0,),
    start_indices_batching_dims=(0,),
)


def pick(table, lanes):
    return lax.gather(table, lanes[..., None], LOOKUP, (1, 1), mode=lax.GatherScatterMode.PROMISE_IN_BOUNDS)


def store_tables(colour_ref, opacity_ref, tab):
    for f in range(2):
        colour = [(colour_ref[f, k : k + 1, :].astype(jnp.float32) / COLOUR_UNIT).astype(jnp.int32) for k in range(3)]
        opacity = (opacity_ref[f : f + 1, :].astype(jnp.float32) / OPACITY_UNIT).astype(jnp.int32)
        for w, word in enumerate((colour[0] + colour[1] * FIELD, colour[2] + opacity * FIELD)):
            for h in range(2):
                tab[f, w, h] = jnp.broadcast_to(word[:, h * LANES : (h + 1) * LANES], (SUBS, LANES))


def masks():
    sub = lax.broadcasted_iota(jnp.int32, (SUBS, LANES), 0)
    lane = lax.broadcasted_iota(jnp.int32, (SUBS, LANES), 1)
    return sub == 0, sub == SUBS - 1, lane == 0, lane == LANES - 1


def cell(at, bins_of, tab, edges):
    first_sub, last_sub, first_lane, last_lane = edges
    colour = clear = None
    for f in range(2):
        here = at(f, 0, 0, 0)
        dz = at(f, 1, 0, 0) - at(f, -1, 0, 0)
        after = pltpu.roll(jnp.where(first_sub, at(f, 0, SUBS, 0), here), SUBS - 1, 0)
        before = pltpu.roll(jnp.where(last_sub, at(f, 0, -SUBS, 0), here), 1, 0)
        dx = after - before
        after = pltpu.roll(jnp.where(first_lane, at(f, 0, 0, LANES), here), LANES - 1, 1)
        before = pltpu.roll(jnp.where(last_lane, at(f, 0, 0, -LANES), here), 1, 1)
        dy = after - before
        total = dz * dz + dx * dx + dy * dy
        shade = 0.3 + (0.35 * jnp.abs(dz)) * lax.rsqrt(0.25 * total + 1.0)
        root = total * lax.rsqrt(jnp.maximum(total, 1e-30))
        gain = 0.25 * OPACITY_UNIT + (0.5 * OPACITY_UNIT) * root
        entry = bins_of(f)
        low = entry & (LANES - 1)
        upper = entry >= LANES
        words = [jnp.where(upper, pick(tab[f, w, 1], low), pick(tab[f, w, 0], low)) for w in range(2)]
        alpha = (words[1] >> 13).astype(jnp.float32) * gain
        lit = alpha * shade
        looked = (words[0] & (FIELD - 1), words[0] >> 13, words[1] & (FIELD - 1))
        terms = [lit * value.astype(jnp.float32) for value in looked]
        colour = terms if colour is None else [a + b for a, b in zip(colour, terms)]
        clear = 1.0 - alpha if clear is None else clear * (1.0 - alpha)
    return colour, clear


def composite(elements, backward):
    colour = through = None
    for part, clear in elements:
        if colour is None:
            colour, through = part, clear
        else:
            keep = jnp.where(backward, clear, 1.0)
            weight = jnp.where(backward, 1.0, through)
            colour = [a * keep + weight * b for a, b in zip(colour, part)]
            through = through * clear
    return colour, through


def inner_kernel(fields, bins, colour, opacity, back, cells, picks, mid, tab, field_sem, bin_sem):
    depth, cols, rows = fields.shape[1:]
    groups = cols // SUBS
    spans = [pl.ds(g * SUBS, SUBS) for g in range(groups)]
    field_copies, bin_copies = [], []
    for g, span in enumerate(spans):
        target = cells.at[:, :, span, pl.ds(LANES, rows)]
        field_copies.append(pltpu.make_async_copy(fields.at[:, :, span, :], target, field_sem.at[g]))
        bin_copies.append(pltpu.make_async_copy(bins.at[:, :, span, :], picks.at[:, :, span, :], bin_sem.at[g]))
    for copy in field_copies[:3] + [bin_copies[1]] + field_copies[3:] + bin_copies[2:] + [bin_copies[0]]:
        copy.start()
    zero = jnp.zeros((cols, LANES), jnp.float32)
    for f in range(2):
        for d in range(depth):
            cells[f, d, :, 0:LANES] = zero
            cells[f, d, :, LANES + rows :] = zero
    store_tables(colour, opacity, tab)
    edges = masks()
    field_copies[0].wait()
    for g in range(1, groups - 1):
        if g == 1:
            field_copies[1].wait()
        field_copies[g + 1].wait()
        bin_copies[g].wait()
        backward = back[g * SUBS : (g + 1) * SUBS, :] == 1

        def tile(b, carry, g=g, backward=backward):
            start = pl.multiple_of(b * LANES, LANES)

            def element(d):
                def at(f, dd, dc, dr):
                    return cells[f, d + dd, pl.ds(g * SUBS + dc, SUBS), pl.ds(start + (LANES + dr), LANES)]

                def bins_of(f):
                    return picks[f, d, pl.ds(g * SUBS, SUBS), pl.ds(start, LANES)]

                return cell(at, bins_of, tab, edges)

            parts, through = composite((element(d) for d in range(1, depth - 1)), backward)
            for k, part in enumerate(parts + [through]):
                mid[b, k, pl.ds((g - 1) * SUBS, SUBS), :] = part
            return carry

        lax.fori_loop(0, rows // LANES, tile, 0)
    bin_copies[0].wait()
    bin_copies[groups - 1].wait()


def outer_kernel(cells, zlo, zhi, xlo, xhi, picks, mid, colour, opacity, back, out, tab):
    depth, cols, rows = picks.shape[1:]
    groups = cols // SUBS
    store_tables(colour, opacity, tab)
    edges = masks()
    for g in range(groups):
        backward = back[g * SUBS : (g + 1) * SUBS, :] == 1
        inside = 0 < g < groups - 1

        def tile(b, carry, g=g, backward=backward, inside=inside):
            start = pl.multiple_of(b * LANES, LANES)
            here = pl.ds(start, LANES)

            def element(d):
                def at(f, dd, dc, dr):
                    if d + dd < 0:
                        return zlo[f, 0, pl.ds(g * SUBS, SUBS), here]
                    if d + dd == depth:
                        return zhi[f, 0, pl.ds(g * SUBS, SUBS), here]
                    if g * SUBS + dc < 0:
                        return jnp.broadcast_to(xlo[f, d, :, here], (SUBS, LANES))
                    if g * SUBS + dc == cols:
                        return jnp.broadcast_to(xhi[f, d, :, here], (SUBS, LANES))
                    return cells[f, d + dd, pl.ds(g * SUBS + dc, SUBS), pl.ds(start + (LANES + dr), LANES)]

                def bins_of(f):
                    return picks[f, d, pl.ds(g * SUBS, SUBS), here]

                return cell(at, bins_of, tab, edges)

            def middle():
                parts = [mid[b, k, pl.ds((g - 1) * SUBS, SUBS), :] for k in range(4)]
                return parts[:3], parts[3]

            if inside:
                elements = (element(0) if n == 0 else middle() if n == 1 else element(depth - 1) for n in range(3))
            else:
                elements = (element(d) for d in range(depth))
            parts, through = composite(elements, backward)
            for k, part in enumerate(parts):
                out[b, k, pl.ds(g * SUBS, SUBS), :] = part * COLOUR_UNIT
            out[b, 3, pl.ds(g * SUBS, SUBS), :] = 1.0 - through
            return carry

        lax.fori_loop(0, rows // LANES, tile, 0)


VMEM = pl.BlockSpec(memory_space=pltpu.VMEM)
SMEM = pl.BlockSpec(memory_space=pltpu.SMEM)
ANY = pl.BlockSpec(memory_space=pl.ANY)
LIMIT = 24 * 2**20


TAB = pltpu.VMEM((2, 2, 2, SUBS, LANES), jnp.int32)


def march_inner(fields, bins, colour, opacity, back):
    _, depth, cols, rows = fields.shape
    within = cols - 2 * SUBS
    return pl.pallas_call(
        inner_kernel,
        out_shape=[
            pltpu.VMEM((2, depth, cols, rows + 2 * LANES), jnp.float32),
            pltpu.VMEM((2, depth, cols, rows), jnp.int32),
            pltpu.VMEM((rows // LANES, 4, within, LANES), jnp.float32),
        ],
        in_specs=[ANY, ANY, VMEM, VMEM, VMEM],
        out_specs=[VMEM] * 3,
        scratch_shapes=[TAB, pltpu.SemaphoreType.DMA((cols // SUBS,)), pltpu.SemaphoreType.DMA((cols // SUBS,))],
        compiler_params=pltpu.CompilerParams(vmem_limit_bytes=LIMIT),
        cost_estimate=pl.CostEstimate(flops=100 * 2 * (depth - 2) * within * rows, bytes_accessed=8 * 2**20, transcendentals=0),
        name="march_inner",
    )(
        pltpu.with_memory_space_constraint(fields, pltpu.HBM),
        pltpu.with_memory_space_constraint(bins, pltpu.HBM),
        colour,
        opacity,
        back,
    )


def march_outer(cells, zlo, zhi, xlo, xhi, picks, mid, colour, opacity, back):
    _, depth, cols, rows = picks.shape
    return pl.pallas_call(
        outer_kernel,
        out_shape=jax.ShapeDtypeStruct((rows // LANES, 4, cols, LANES), jnp.float32),
        in_specs=[VMEM] * 10,
        out_specs=VMEM,
        scratch_shapes=[TAB],
        compiler_params=pltpu.CompilerParams(vmem_limit_bytes=LIMIT),
        name="march_outer",
    )(cells, zlo, zhi, xlo, xhi, picks, mid, colour, opacity, back)


def join_kernel(parts, back, out):
    depth, _, cols, _ = parts.shape
    for group in range(cols // SUBS):
        span = pl.ds(group * SUBS, SUBS)
        elements = (([parts[d, k, span, :] for k in range(3)], 1.0 - parts[d, 3, span, :]) for d in range(depth))
        colour, through = composite(elements, back[span, :] == 1)
        for k in range(3):
            out[k, span, :] = colour[k]
        out[3, span, :] = 1.0 - through


def join(parts, back):
    return pl.pallas_call(
        join_kernel,
        out_shape=jax.ShapeDtypeStruct(parts.shape[1:], jnp.float32),
        in_specs=[VMEM, VMEM],
        out_specs=VMEM,
        name="join",
    )(parts, back)


def place_kernel(spots, *refs):
    pieces, out = refs[:-1], refs[-1]
    x_count = len(pieces) // 2
    channel = pl.program_id(0)
    for n, piece in enumerate(pieces):
        x, c = spots[n % x_count], spots[x_count + n // x_count]
        for high in range(2):
            for mid in range(2):
                for low in range(2):
                    out[0, 4 * high + 2 * mid + low, x, c] = piece[low, mid, high, channel]


def place(pieces, others, spots):
    x_count = len(pieces)
    channels, cols, rows = pieces[0].shape[3:]
    whole = (channels, 8, x_count, 2, cols, rows)
    frame = pl.pallas_call(
        place_kernel,
        grid=(channels,),
        out_shape=jax.ShapeDtypeStruct(whole, jnp.float32),
        in_specs=[SMEM] + [VMEM] * (2 * x_count),
        out_specs=pl.BlockSpec((1,) + whole[1:], lambda channel: (channel, 0, 0, 0, 0, 0)),
        compiler_params=pltpu.CompilerParams(vmem_limit_bytes=LIMIT),
        name="place",
    )(spots, *pieces, *others)
    return frame.reshape(channels, 16 * x_count * cols, rows)


def shifted(value, axis, step, wrap=True):
    count = lax.axis_size(axis)
    route = [(i, (i + step) % count) for i in range(count) if wrap or 0 <= i + step < count]
    return lax.ppermute(value, axis, route)


WIDE = ("z_high", "z_mid", "z_low", "x", "core")


def on_device(fields, field_bins, colour_table, opacity_table, view_dir):
    depth, cols = fields.shape[1:3]
    zlo = shifted(fields[:, depth - 1 :], "y", 1, wrap=False)
    zhi = shifted(fields[:, :1], "y", -1, wrap=False)
    xlo = shifted(fields[:, :, cols - 1 :], WIDE, 1, wrap=False)
    xhi = shifted(fields[:, :, :1], WIDE, -1, wrap=False)
    back = jnp.broadcast_to(view_dir[:, None], (cols, LANES))
    cells, picks, mid = march_inner(fields, field_bins, colour_table, opacity_table, back)
    partial = march_outer(cells, zlo, zhi, xlo, xhi, picks, mid, colour_table, opacity_table, back)
    partial = lax.all_to_all(partial, "y", 0, 0)
    column = join(partial, back)
    for axis in ("z_high", "z_mid", "z_low"):
        column = lax.all_gather(column, axis)
    x_count = lax.axis_size("x")
    steps = [0, 1, x_count - 1] + list(range(2, x_count - 1))
    pieces = [column] + [shifted(column, "x", -step) for step in steps[1:]]
    others = [lax.ppermute(piece, "core", [(0, 1), (1, 0)]) for piece in pieces]
    x, core = lax.axis_index("x"), lax.axis_index("core")
    spots = jnp.stack([(x + step) % x_count for step in steps] + [core, 1 - core])
    return place(pieces, others, spots)


def solution(mesh):
    grid = Mesh(mesh.devices.reshape(2, 2, 2, 4, 2, 8), WIDE + ("y",))
    split = P(None, "y", WIDE, None)
    return jax.shard_map(
        on_device,
        mesh=grid,
        in_specs=(split, split, P(), P(), P(WIDE)),
        out_specs=P(None, None, "y"),
        check_vma=False,
    )
```

```python
import jax
import jax.numpy as jnp
from jax import lax
from jax.experimental import pallas as pl
from jax.experimental.pallas import tpu as pltpu
from jax.sharding import Mesh, PartitionSpec as P

LANES = 128
SUBS = 8
COLOUR_UNIT = 2.0**-12
OPACITY_UNIT = 2.0**-18
FIELD = 1 << 13

LOOKUP = lax.GatherDimensionNumbers(
    offset_dims=(),
    collapsed_slice_dims=(1,),
    start_index_map=(1,),
    operand_batching_dims=(0,),
    start_indices_batching_dims=(0,),
)


def pick(table, lanes):
    return lax.gather(table, lanes[..., None], LOOKUP, (1, 1), mode=lax.GatherScatterMode.PROMISE_IN_BOUNDS)


def store_tables(colour_ref, opacity_ref, tab):
    for f in range(2):
        colour = [(colour_ref[k, f : f + 1, :].astype(jnp.float32) / COLOUR_UNIT).astype(jnp.int32) for k in range(3)]
        opacity = (opacity_ref[f : f + 1, :].astype(jnp.float32) / OPACITY_UNIT).astype(jnp.int32)
        for w, word in enumerate((colour[0] + colour[1] * FIELD, colour[2] + opacity * FIELD)):
            for h in range(2):
                tab[f, w, h] = jnp.broadcast_to(word[:, h * LANES : (h + 1) * LANES], (SUBS, LANES))


def masks():
    sub = lax.broadcasted_iota(jnp.int32, (SUBS, LANES), 0)
    lane = lax.broadcasted_iota(jnp.int32, (SUBS, LANES), 1)
    return sub == 0, sub == SUBS - 1, lane == 0, lane == LANES - 1


def cell(at, bins_of, d, tab, edges):
    first_sub, last_sub, first_lane, last_lane = edges
    colour = clear = None
    for f in range(2):
        here = at(f, d, 0, 0)
        dz = at(f, d + 1, 0, 0) - at(f, d - 1, 0, 0)
        after = pltpu.roll(jnp.where(first_sub, at(f, d, SUBS, 0), here), SUBS - 1, 0)
        before = pltpu.roll(jnp.where(last_sub, at(f, d, -SUBS, 0), here), 1, 0)
        dx = after - before
        after = pltpu.roll(jnp.where(first_lane, at(f, d, 0, LANES), here), LANES - 1, 1)
        before = pltpu.roll(jnp.where(last_lane, at(f, d, 0, -LANES), here), 1, 1)
        dy = after - before
        total = dz * dz + dx * dx + dy * dy
        shade = 0.3 + (0.35 * jnp.abs(dz)) * lax.rsqrt(0.25 * total + 1.0)
        root = total * lax.rsqrt(jnp.maximum(total, 1e-30))
        gain = 0.25 * OPACITY_UNIT + (0.5 * OPACITY_UNIT) * root
        entry = bins_of(f)
        low = entry & (LANES - 1)
        upper = entry >= LANES
        words = [jnp.where(upper, pick(tab[f, w, 1], low), pick(tab[f, w, 0], low)) for w in range(2)]
        alpha = (words[1] >> 13).astype(jnp.float32) * gain
        lit = alpha * shade
        looked = (words[0] & (FIELD - 1), words[0] >> 13, words[1] & (FIELD - 1))
        terms = [lit * value.astype(jnp.float32) for value in looked]
        colour = terms if colour is None else [a + b for a, b in zip(colour, terms)]
        clear = 1.0 - alpha if clear is None else clear * (1.0 - alpha)
    return colour, clear


def composite(elements, backward):
    colour = through = None
    for part, clear in elements:
        if colour is None:
            colour, through = part, clear
        else:
            keep = jnp.where(backward, clear, 1.0)
            weight = jnp.where(backward, 1.0, through)
            colour = [a * keep + weight * b for a, b in zip(colour, part)]
            through = through * clear
    return colour, through


def lattice(cells, xlo, xhi, zlo, zhi, g, start):
    _, depth, cols, _ = cells.shape
    span, here = pl.ds(g * SUBS, SUBS), pl.ds(start, LANES)

    def at(f, d, dc, dr):
        if d < 0:
            return zlo[f, 0, span, here]
        if d == depth:
            return zhi[f, 0, span, here]
        if g * SUBS + dc < 0:
            return jnp.broadcast_to(xlo[f, d, :, here], (SUBS, LANES))
        if g * SUBS + dc == cols:
            return jnp.broadcast_to(xhi[f, d, :, here], (SUBS, LANES))
        return cells[f, d, pl.ds(g * SUBS + dc, SUBS), pl.ds(start + (LANES + dr), LANES)]

    return at


def inner_kernel(
    fields, bins, xlo, xhi, colour, opacity, view, cells, picks, mid, tab, back, colour_now, opacity_now, field_sem, bin_sem, tab_sem
):
    depth, cols, rows = fields.shape[1:]
    groups = cols // SUBS
    spans = [pl.ds(g * SUBS, SUBS) for g in range(groups)]
    tab_copies = [
        pltpu.make_async_copy(colour, colour_now, tab_sem.at[0]),
        pltpu.make_async_copy(opacity, opacity_now, tab_sem.at[1]),
    ]
    field_copies, bin_copies = [], []
    for g, span in enumerate(spans):
        target = cells.at[:, :, span, pl.ds(LANES, rows)]
        field_copies.append(pltpu.make_async_copy(fields.at[:, :, span, :], target, field_sem.at[g]))
        bin_copies.append(pltpu.make_async_copy(bins.at[:, :, span, :], picks.at[:, :, span, :], bin_sem.at[g]))
    for copy in tab_copies + [field_copies[0], bin_copies[0], field_copies[1]]:
        copy.start()
    for g in range(1, groups):
        bin_copies[g].start()
        if g + 1 < groups:
            field_copies[g + 1].start()
    zero = jnp.zeros((cols, LANES), jnp.float32)
    for f in range(2):
        for d in range(depth):
            cells[f, d, :, 0:LANES] = zero
            cells[f, d, :, LANES + rows :] = zero
    sub = lax.broadcasted_iota(jnp.int32, (SUBS, LANES), 0)
    for g in range(groups):
        towards = jnp.zeros((SUBS, LANES), jnp.int32)
        for k in range(SUBS):
            towards = jnp.where(sub == k, view[g * SUBS + k], towards)
        back[g * SUBS : (g + 1) * SUBS, :] = towards
    for copy in tab_copies:
        copy.wait()
    store_tables(colour_now, opacity_now, tab)
    edges = masks()
    field_copies[0].wait()
    for g in range(groups):
        if g + 1 < groups:
            field_copies[g + 1].wait()
        bin_copies[g].wait()
        backward = back[g * SUBS : (g + 1) * SUBS, :] == 1

        def tile(b, carry, g=g, backward=backward):
            start = pl.multiple_of(b * LANES, LANES)
            at = lattice(cells, xlo, xhi, None, None, g, start)

            def element(d):
                return cell(at, lambda f: picks[f, d, pl.ds(g * SUBS, SUBS), pl.ds(start, LANES)], d, tab, edges)

            parts, through = composite((element(d) for d in range(1, depth - 1)), backward)
            for k, part in enumerate(parts + [through]):
                mid[b, k, pl.ds(g * SUBS, SUBS), :] = part
            return carry

        lax.fori_loop(0, rows // LANES, tile, 0, unroll=4)


def outer_kernel(cells, zlo, zhi, xlo, xhi, picks, mid, tab, back, out):
    depth, cols, rows = picks.shape[1:]
    edges = masks()
    for g in range(cols // SUBS):
        backward = back[g * SUBS : (g + 1) * SUBS, :] == 1

        def tile(b, carry, g=g, backward=backward):
            start = pl.multiple_of(b * LANES, LANES)
            at = lattice(cells, xlo, xhi, zlo, zhi, g, start)

            def element(d):
                return cell(at, lambda f: picks[f, d, pl.ds(g * SUBS, SUBS), pl.ds(start, LANES)], d, tab, edges)

            middle = [mid[b, k, pl.ds(g * SUBS, SUBS), :] for k in range(4)]
            elements = [element(0), (middle[:3], middle[3]), element(depth - 1)]
            parts, through = composite(elements, backward)
            for k, part in enumerate(parts):
                out[b, k, pl.ds(g * SUBS, SUBS), :] = part * COLOUR_UNIT
            out[b, 3, pl.ds(g * SUBS, SUBS), :] = 1.0 - through
            return carry

        lax.fori_loop(0, rows // LANES, tile, 0, unroll=8)


VMEM = pl.BlockSpec(memory_space=pltpu.VMEM)
SMEM = pl.BlockSpec(memory_space=pltpu.SMEM)
ANY = pl.BlockSpec(memory_space=pl.ANY)
LIMIT = 24 * 2**20


def march_inner(fields, bins, xlo, xhi, colour, opacity, view):
    _, depth, cols, rows = fields.shape
    resident = [pltpu.with_memory_space_constraint(x, pltpu.HBM) for x in (fields, bins)]
    tables = [pltpu.with_memory_space_constraint(x, pltpu.HBM) for x in (colour, opacity)]
    return pl.pallas_call(
        inner_kernel,
        out_shape=[
            pltpu.VMEM((2, depth, cols, rows + 2 * LANES), jnp.float32),
            pltpu.VMEM((2, depth, cols, rows), jnp.int32),
            pltpu.VMEM((rows // LANES, 4, cols, LANES), jnp.float32),
            pltpu.VMEM((2, 2, 2, SUBS, LANES), jnp.int32),
            pltpu.VMEM((cols, LANES), jnp.int32),
        ],
        in_specs=[ANY, ANY, VMEM, VMEM, ANY, ANY, SMEM],
        out_specs=[VMEM] * 5,
        scratch_shapes=[
            pltpu.VMEM(colour.shape, colour.dtype),
            pltpu.VMEM(opacity.shape, opacity.dtype),
            pltpu.SemaphoreType.DMA((cols // SUBS,)),
            pltpu.SemaphoreType.DMA((cols // SUBS,)),
            pltpu.SemaphoreType.DMA((2,)),
        ],
        compiler_params=pltpu.CompilerParams(vmem_limit_bytes=LIMIT),
        cost_estimate=pl.CostEstimate(flops=100 * 2 * depth * cols * rows, bytes_accessed=8 * 2**20, transcendentals=0),
        name="march_inner",
    )(*resident, xlo, xhi, *tables, view)


def march_outer(cells, zlo, zhi, xlo, xhi, picks, mid, tab, back):
    _, depth, cols, rows = picks.shape
    return pl.pallas_call(
        outer_kernel,
        out_shape=pltpu.VMEM((rows // LANES, 4, cols, LANES), jnp.float32),
        in_specs=[VMEM] * 9,
        out_specs=VMEM,
        compiler_params=pltpu.CompilerParams(vmem_limit_bytes=LIMIT),
        name="march_outer",
    )(cells, zlo, zhi, xlo, xhi, picks, mid, tab, back)


def join_kernel(parts, back, out):
    depth, _, cols, _ = parts.shape
    for group in range(cols // SUBS):
        span = pl.ds(group * SUBS, SUBS)
        elements = (([parts[d, k, span, :] for k in range(3)], 1.0 - parts[d, 3, span, :]) for d in range(depth))
        colour, through = composite(elements, back[span, :] == 1)
        for k in range(3):
            out[k, span, :] = colour[k]
        out[3, span, :] = 1.0 - through


def join(parts, back):
    return pl.pallas_call(
        join_kernel,
        out_shape=jax.ShapeDtypeStruct(parts.shape[1:], jnp.float32),
        in_specs=[VMEM, VMEM],
        out_specs=VMEM,
        name="join",
    )(parts, back)


def place_kernel(core, pieces, *refs):
    out = refs[-1]
    channel = pl.program_id(0)
    for x in range(pieces.shape[0]):
        for high in range(2):
            for mid in range(2):
                for low in range(2):
                    out[0, 4 * high + 2 * mid + low, x, 0] = pieces[x, low, mid, high, channel]


def place(pieces, core, frame=None):
    x_count = pieces.shape[0]
    channels, cols, rows = pieces.shape[4:]
    whole = (channels, 8, x_count, 2, cols, rows)
    block = (1, 8, x_count, 1, cols, rows)
    kept = [] if frame is None else [frame]
    return pl.pallas_call(
        place_kernel,
        grid_spec=pltpu.PrefetchScalarGridSpec(
            num_scalar_prefetch=1,
            grid=(channels,),
            in_specs=[VMEM] + [ANY] * len(kept),
            out_specs=pl.BlockSpec(block, lambda channel, core: (channel, 0, 0, core[0], 0, 0)),
        ),
        out_shape=jax.ShapeDtypeStruct(whole, jnp.float32),
        input_output_aliases={2: 0} if kept else {},
        compiler_params=pltpu.CompilerParams(vmem_limit_bytes=LIMIT),
        cost_estimate=pl.CostEstimate(flops=0, bytes_accessed=4 * 2**20, transcendentals=0),
        name="place",
    )(core.reshape(1), pieces, *kept)


def shifted(value, axis, step, wrap=True):
    count = lax.axis_size(axis)
    route = [(i, (i + step) % count) for i in range(count) if wrap or 0 <= i + step < count]
    return lax.ppermute(value, axis, route)


WIDE = ("z_high", "z_mid", "z_low", "x", "core")


def on_device(fields, field_bins, colour_table, opacity_table, view_dir):
    depth, cols = fields.shape[1:3]
    xlo = shifted(fields[:, :, cols - 1 :], WIDE, 1, wrap=False)
    xhi = shifted(fields[:, :, :1], WIDE, -1, wrap=False)
    zlo = shifted(fields[:, depth - 1 :], "y", 1, wrap=False)
    zhi = shifted(fields[:, :1], "y", -1, wrap=False)
    colour = jnp.transpose(colour_table, (1, 0, 2))
    cells, picks, mid, tab, back = march_inner(fields, field_bins, xlo, xhi, colour, opacity_table, view_dir)
    partial = march_outer(cells, zlo, zhi, xlo, xhi, picks, mid, tab, back)
    partial = lax.all_to_all(partial, "y", 0, 0)
    column = join(partial, back)
    for axis in ("z_high", "z_mid", "z_low"):
        column = lax.all_gather(column, axis)
    x_count = lax.axis_size("x")
    own = lax.all_to_all(jnp.broadcast_to(column[None], (x_count,) + column.shape), "x", 0, 0)
    other = lax.ppermute(own, "core", [(0, 1), (1, 0)])
    core = lax.axis_index("core").astype(jnp.int32)
    frame = place(other, 1 - core, place(own, core))
    channels, _, _, _, _, rows = frame.shape
    return frame.reshape(channels, -1, rows)


def solution(mesh):
    grid = Mesh(mesh.devices.reshape(2, 2, 2, 4, 2, 8), WIDE + ("y",))
    split = P(None, "y", WIDE, None)
    return jax.shard_map(
        on_device,
        mesh=grid,
        in_specs=(split, split, P(), P(), P(WIDE)),
        out_specs=P(None, None, "y"),
        check_vma=False,
    )
```

```python
import functools

import jax
import jax.numpy as jnp
from jax import lax
from jax.experimental import pallas as pl
from jax.experimental.pallas import tpu as pltpu
from jax.sharding import PartitionSpec as P

LANES = 128
SUBS = 8
COLOUR_UNIT = 2.0**-12
OPACITY_UNIT = 2.0**-18
FIELD = 1 << 13

LOOKUP = lax.GatherDimensionNumbers(
    offset_dims=(),
    collapsed_slice_dims=(1,),
    start_index_map=(1,),
    operand_batching_dims=(0,),
    start_indices_batching_dims=(0,),
)


def pick(table, lanes):
    return lax.gather(table, lanes[..., None], LOOKUP, (1, 1), mode=lax.GatherScatterMode.PROMISE_IN_BOUNDS)


def store_tables(colour_ref, opacity_ref, tab):
    for f in range(2):
        colour = [(colour_ref[k, f : f + 1, :].astype(jnp.float32) / COLOUR_UNIT).astype(jnp.int32) for k in range(3)]
        opacity = (opacity_ref[f : f + 1, :].astype(jnp.float32) / OPACITY_UNIT).astype(jnp.int32)
        for w, word in enumerate((colour[0] + colour[1] * FIELD, colour[2] + opacity * FIELD)):
            for h in range(2):
                tab[f, w, h] = jnp.broadcast_to(word[:, h * LANES : (h + 1) * LANES], (SUBS, LANES))


def masks():
    sub = lax.broadcasted_iota(jnp.int32, (SUBS, LANES), 0)
    lane = lax.broadcasted_iota(jnp.int32, (SUBS, LANES), 1)
    return sub == 0, sub == SUBS - 1, lane == 0, lane == LANES - 1


def cell(at, bins_of, d, tab, edges):
    first_sub, last_sub, first_lane, last_lane = edges
    colour = clear = None
    for f in range(2):
        here = at(f, d, 0, 0)
        dz = at(f, d + 1, 0, 0) - at(f, d - 1, 0, 0)
        after = pltpu.roll(jnp.where(first_sub, at(f, d, SUBS, 0), here), SUBS - 1, 0)
        before = pltpu.roll(jnp.where(last_sub, at(f, d, -SUBS, 0), here), 1, 0)
        dx = after - before
        after = pltpu.roll(jnp.where(first_lane, at(f, d, 0, LANES), here), LANES - 1, 1)
        before = pltpu.roll(jnp.where(last_lane, at(f, d, 0, -LANES), here), 1, 1)
        dy = after - before
        total = dz * dz + dx * dx + dy * dy
        shade = 0.3 + (0.35 * jnp.abs(dz)) * lax.rsqrt(0.25 * total + 1.0)
        root = total * lax.rsqrt(jnp.maximum(total, 1e-30))
        gain = 0.25 * OPACITY_UNIT + (0.5 * OPACITY_UNIT) * root
        entry = bins_of(f)
        low = entry & (LANES - 1)
        upper = entry >= LANES
        words = [jnp.where(upper, pick(tab[f, w, 1], low), pick(tab[f, w, 0], low)) for w in range(2)]
        alpha = (words[1] >> 13).astype(jnp.float32) * gain
        lit = alpha * shade
        looked = (words[0] & (FIELD - 1), words[0] >> 13, words[1] & (FIELD - 1))
        terms = [lit * value.astype(jnp.float32) for value in looked]
        colour = terms if colour is None else [a + b for a, b in zip(colour, terms)]
        clear = 1.0 - alpha if clear is None else clear * (1.0 - alpha)
    return colour, clear


def composite(elements, backward):
    colour = through = None
    for part, clear in elements:
        if colour is None:
            colour, through = part, clear
        else:
            keep = jnp.where(backward, clear, 1.0)
            weight = jnp.where(backward, 1.0, through)
            colour = [a * keep + weight * b for a, b in zip(colour, part)]
            through = through * clear
    return colour, through


def lattice(cells, xlo, xhi, zlo, zhi, g, start):
    _, depth, cols, _ = cells.shape
    span, here = pl.ds(g * SUBS, SUBS), pl.ds(start, LANES)

    def at(f, d, dc, dr):
        if d < 0:
            return zlo[f, 0, span, here]
        if d == depth:
            return zhi[f, 0, span, here]
        if g * SUBS + dc < 0:
            return jnp.broadcast_to(xlo[f, d, :, here], (SUBS, LANES))
        if g * SUBS + dc == cols:
            return jnp.broadcast_to(xhi[f, d, :, here], (SUBS, LANES))
        return cells[f, d, pl.ds(g * SUBS + dc, SUBS), pl.ds(start + (LANES + dr), LANES)]

    return at


def inner_kernel(
    fields, bins, xlo, xhi, colour, opacity, view, cells, picks, mid, tab, back, colour_now, opacity_now, view_now, field_sem, bin_sem, tab_sem
):
    depth, cols, rows = fields.shape[1:]
    groups, half = cols // SUBS, rows // 2
    small = [
        pltpu.make_async_copy(source, target, tab_sem.at[n])
        for n, (source, target) in enumerate(((colour, colour_now), (opacity, opacity_now), (view, view_now)))
    ]
    parts = (pl.ds(0, half + LANES), pl.ds(half + LANES, half - LANES))
    field_copies, bin_copies = {}, {}
    for g in range(groups):
        span = pl.ds(g * SUBS, SUBS)
        for h, part in enumerate(parts):
            target = cells.at[:, :, span, pl.ds(LANES + part.start, part.size)]
            field_copies[g, h] = pltpu.make_async_copy(fields.at[:, :, span, part], target, field_sem.at[g, h])
            part = pl.ds(h * half, half)
            bin_copies[g, h] = pltpu.make_async_copy(bins.at[:, :, span, part], picks.at[:, :, span, part], bin_sem.at[g, h])
    for copy in small:
        copy.start()
    for g in range(groups):
        for h in range(2):
            if g == 0:
                field_copies[g, h].start()
            if g + 1 < groups:
                field_copies[g + 1, h].start()
            bin_copies[g, h].start()
    zero = jnp.zeros((cols, LANES), jnp.float32)
    for f in range(2):
        for d in range(depth):
            cells[f, d, :, 0:LANES] = zero
            cells[f, d, :, LANES + rows :] = zero
    for copy in small:
        copy.wait()
    sub = lax.broadcasted_iota(jnp.int32, (SUBS, LANES), 0)
    for g in range(groups):
        towards = jnp.zeros((SUBS, LANES), jnp.int32)
        for k in range(SUBS):
            towards = jnp.where(sub == k, view_now[g * SUBS + k], towards)
        back[g * SUBS : (g + 1) * SUBS, :] = towards
    store_tables(colour_now, opacity_now, tab)
    edges = masks()
    for g in range(groups):
        backward = back[g * SUBS : (g + 1) * SUBS, :] == 1

        def tile(b, carry, g=g, backward=backward):
            start = pl.multiple_of(b * LANES, LANES)
            at = lattice(cells, xlo, xhi, None, None, g, start)

            def element(d):
                return cell(at, lambda f: picks[f, d, pl.ds(g * SUBS, SUBS), pl.ds(start, LANES)], d, tab, edges)

            colours, through = composite((element(d) for d in range(1, depth - 1)), backward)
            for k, value in enumerate(colours + [through]):
                mid[b, k, pl.ds(g * SUBS, SUBS), :] = value
            return carry

        for h in range(2):
            if g == 0:
                field_copies[g, h].wait()
            if g + 1 < groups:
                field_copies[g + 1, h].wait()
            bin_copies[g, h].wait()
            lax.fori_loop(h * half // LANES, (h + 1) * half // LANES, tile, 0, unroll=4)


def outer_kernel(cells, zlo, zhi, xlo, xhi, picks, mid, tab, back, out):
    depth, cols, rows = picks.shape[1:]
    edges = masks()
    for g in range(cols // SUBS):
        backward = back[g * SUBS : (g + 1) * SUBS, :] == 1

        def tile(b, carry, g=g, backward=backward):
            start = pl.multiple_of(b * LANES, LANES)
            at = lattice(cells, xlo, xhi, zlo, zhi, g, start)

            def element(d):
                return cell(at, lambda f: picks[f, d, pl.ds(g * SUBS, SUBS), pl.ds(start, LANES)], d, tab, edges)

            middle = [mid[b, k, pl.ds(g * SUBS, SUBS), :] for k in range(4)]
            elements = [element(0), (middle[:3], middle[3]), element(depth - 1)]
            parts, through = composite(elements, backward)
            for k, part in enumerate(parts):
                out[b, k, pl.ds(g * SUBS, SUBS), :] = part * COLOUR_UNIT
            out[b, 3, pl.ds(g * SUBS, SUBS), :] = 1.0 - through
            return carry

        lax.fori_loop(0, rows // LANES, tile, 0, unroll=8)


VMEM = pl.BlockSpec(memory_space=pltpu.VMEM)
SMEM = pl.BlockSpec(memory_space=pltpu.SMEM)
ANY = pl.BlockSpec(memory_space=pl.ANY)
LIMIT = 24 * 2**20


def march_inner(fields, bins, xlo, xhi, colour, opacity, view):
    _, depth, cols, rows = fields.shape
    resident = [pltpu.with_memory_space_constraint(x, pltpu.HBM) for x in (fields, bins)]
    tables = [pltpu.with_memory_space_constraint(x, pltpu.HBM) for x in (colour, opacity, view)]
    return pl.pallas_call(
        inner_kernel,
        out_shape=[
            pltpu.VMEM((2, depth, cols, rows + 2 * LANES), jnp.float32),
            pltpu.VMEM((2, depth, cols, rows), jnp.int32),
            pltpu.VMEM((rows // LANES, 4, cols, LANES), jnp.float32),
            pltpu.VMEM((2, 2, 2, SUBS, LANES), jnp.int32),
            pltpu.VMEM((cols, LANES), jnp.int32),
        ],
        in_specs=[ANY, ANY, VMEM, VMEM, ANY, ANY, ANY],
        out_specs=[VMEM] * 5,
        scratch_shapes=[
            pltpu.VMEM(colour.shape, colour.dtype),
            pltpu.VMEM(opacity.shape, opacity.dtype),
            pltpu.SMEM(view.shape, view.dtype),
            pltpu.SemaphoreType.DMA((cols // SUBS, 2)),
            pltpu.SemaphoreType.DMA((cols // SUBS, 2)),
            pltpu.SemaphoreType.DMA((3,)),
        ],
        compiler_params=pltpu.CompilerParams(vmem_limit_bytes=LIMIT),
        cost_estimate=pl.CostEstimate(flops=50_000 * 2 * depth * cols * rows, bytes_accessed=64 * 2**20, transcendentals=0),
        name="march_inner",
    )(*resident, xlo, xhi, *tables)


def march_outer(cells, zlo, zhi, xlo, xhi, picks, mid, tab, back):
    _, depth, cols, rows = picks.shape
    return pl.pallas_call(
        outer_kernel,
        out_shape=pltpu.VMEM((rows // LANES, 4, cols, LANES), jnp.float32),
        in_specs=[VMEM] * 9,
        out_specs=VMEM,
        compiler_params=pltpu.CompilerParams(vmem_limit_bytes=LIMIT),
        name="march_outer",
    )(cells, zlo, zhi, xlo, xhi, picks, mid, tab, back)


def join_kernel(parts, back, out):
    depth, _, cols, _ = parts.shape
    for group in range(cols // SUBS):
        span = pl.ds(group * SUBS, SUBS)
        elements = (([parts[d, k, span, :] for k in range(3)], 1.0 - parts[d, 3, span, :]) for d in range(depth))
        colour, through = composite(elements, back[span, :] == 1)
        for k in range(3):
            out[k, span, :] = colour[k]
        out[3, span, :] = 1.0 - through


def join(parts, back):
    return pl.pallas_call(
        join_kernel,
        out_shape=pltpu.VMEM(parts.shape[1:], jnp.float32),
        in_specs=[VMEM, VMEM],
        out_specs=VMEM,
        name="join",
    )(pltpu.with_memory_space_constraint(parts, pltpu.VMEM), back)


Z, X, CORES = 8, 4, 2


def device(z, x, core):
    return (z % Z * X + x % X) * CORES + core


def everywhere(target):
    places = [(z, x, core) for z in range(Z) for x in range(X) for core in range(CORES)]
    return [(device(*spot), device(*target(*spot))) for spot in places]


def pairs(partner):
    return [list(pair) for pair in everywhere(partner) if pair[0] < pair[1]]


DOUBLINGS = (
    pairs(lambda z, x, core: (z, x ^ 2, core) if core else (z ^ 4, x, core)),
    pairs(lambda z, x, core: (z, x ^ 1, core) if core else (z ^ 2, x, core)),
    pairs(lambda z, x, core: (z ^ 4, x, core) if core else (z ^ 1, x, core)),
)
MOVES = (
    everywhere(lambda z, x, core: (z + 1, x, core) if core else (z, x + 1, core)),
    everywhere(lambda z, x, core: (z - 1, x, core) if core else (z, x - 1, core)),
    everywhere(lambda z, x, core: (z - 2 if z % 2 else z + 2, x, core) if core else (z, x + 2, core)),
)
STEPS = (0, 1, -1, 2)
SWAP = everywhere(lambda z, x, core: (z, x, 1 - core))


def gather(block):
    for groups in DOUBLINGS:
        block = lax.all_gather(block, "wide", axis_index_groups=groups)
    return [block] + [lax.ppermute(block, "wide", move) for move in MOVES]


def place_kernel(swapped, spot, *refs):
    pieces, out = refs[: len(STEPS)], refs[-1]
    channel = pl.program_id(0)
    wide = spot[0]
    core = (wide + swapped) % CORES
    x, z = wide // CORES % X, wide // (CORES * X)
    for piece, step in enumerate(STEPS):
        x_from, z_from = (x + X - step) % X, (z + Z - step) % (Z // 2)
        for third in range(2):
            for second in range(2):
                for first in range(2):
                    z_zero, x_zero = 4 * first + 2 * second + third, x_from
                    z_one, x_one = 4 * third + z_from, 2 * first + second
                    z_now = jnp.where(core == 0, z_zero, z_one)
                    x_now = jnp.where(core == 0, x_zero, x_one)
                    out[0, z_now, x_now, 0] = pieces[piece][third, second, first, channel]


def place(pieces, spot, swapped, frame=None):
    channels, cols, rows = pieces[0].shape[3:]
    kept = [] if frame is None else [frame]
    return pl.pallas_call(
        functools.partial(place_kernel, swapped),
        grid_spec=pltpu.PrefetchScalarGridSpec(
            num_scalar_prefetch=1,
            grid=(channels,),
            in_specs=[VMEM] * len(pieces) + [ANY] * len(kept),
            out_specs=pl.BlockSpec(
                (1, Z, X, 1, cols, rows), lambda channel, spot: (channel, 0, 0, (spot[0] + swapped) % CORES, 0, 0)
            ),
        ),
        out_shape=jax.ShapeDtypeStruct((channels, Z, X, CORES, cols, rows), jnp.float32),
        input_output_aliases={1 + len(pieces): 0} if kept else {},
        compiler_params=pltpu.CompilerParams(vmem_limit_bytes=LIMIT),
        cost_estimate=pl.CostEstimate(flops=0, bytes_accessed=4 * 2**20, transcendentals=0),
        name="place",
    )(spot, *(pltpu.with_memory_space_constraint(piece, pltpu.VMEM) for piece in pieces), *kept)


def shifted(value, axis, step, wrap=True):
    count = lax.axis_size(axis)
    route = [(i, (i + step) % count) for i in range(count) if wrap or 0 <= i + step < count]
    return lax.ppermute(value, axis, route)


def on_device(fields, field_bins, colour_table, opacity_table, view_dir):
    depth, cols = fields.shape[1:3]
    left, right, fields_after = lax.optimization_barrier((fields[:, :, :1], fields[:, :, cols - 1 :], fields))
    xlo = shifted(right, "wide", 1, wrap=False)
    xhi = shifted(left, "wide", -1, wrap=False)
    zlo = shifted(fields_after[:, depth - 1 :], "narrow", 1, wrap=False)
    zhi = shifted(fields_after[:, :1], "narrow", -1, wrap=False)
    colour = jnp.transpose(colour_table, (1, 0, 2))
    cells, picks, mid, tab, back = march_inner(fields, field_bins, xlo, xhi, colour, opacity_table, view_dir)
    partial = march_outer(cells, zlo, zhi, xlo, xhi, picks, mid, tab, back)
    partial = lax.all_to_all(partial, "narrow", 0, 0)
    own = gather(join(partial, back))
    other = [lax.ppermute(piece, "wide", SWAP) for piece in own]
    spot = lax.axis_index("wide").reshape(1)
    frame = place(other, spot, 1, place(own, spot, 0))
    return frame.reshape(frame.shape[0], -1, frame.shape[-1])


def solution(mesh):
    split = P(None, "narrow", "wide", None)
    return jax.shard_map(
        on_device,
        mesh=mesh,
        in_specs=(split, split, P(), P(), P("wide")),
        out_specs=P(None, None, "narrow"),
        check_vma=False,
    )
```

```python
import functools

import jax
import jax.numpy as jnp
from jax import lax
from jax.experimental import pallas as pl
from jax.experimental.pallas import tpu as pltpu
from jax.sharding import PartitionSpec as P

LANES = 128
SUBS = 8
COLOUR_UNIT = 2.0**-12
OPACITY_UNIT = 2.0**-18
FIELD = 1 << 13

LOOKUP = lax.GatherDimensionNumbers(
    offset_dims=(),
    collapsed_slice_dims=(1,),
    start_index_map=(1,),
    operand_batching_dims=(0,),
    start_indices_batching_dims=(0,),
)


def pick(table, lanes):
    return lax.gather(table, lanes[..., None], LOOKUP, (1, 1), mode=lax.GatherScatterMode.PROMISE_IN_BOUNDS)


def store_tables(colour_ref, opacity_ref, tab):
    for f in range(2):
        colour = [(colour_ref[k, f : f + 1, :].astype(jnp.float32) / COLOUR_UNIT).astype(jnp.int32) for k in range(3)]
        opacity = (opacity_ref[f : f + 1, :].astype(jnp.float32) / OPACITY_UNIT).astype(jnp.int32)
        for w, word in enumerate((colour[0] + colour[1] * FIELD, colour[2] + opacity * FIELD)):
            for h in range(2):
                tab[f, w, h] = jnp.broadcast_to(word[:, h * LANES : (h + 1) * LANES], (SUBS, LANES))


def masks():
    sub = lax.broadcasted_iota(jnp.int32, (SUBS, LANES), 0)
    lane = lax.broadcasted_iota(jnp.int32, (SUBS, LANES), 1)
    return sub == 0, sub == SUBS - 1, lane == 0, lane == LANES - 1


def cell(at, bins_of, d, tab, edges):
    first_sub, last_sub, first_lane, last_lane = edges
    colour = clear = None
    for f in range(2):
        here = at(f, d, 0, 0)
        dz = at(f, d + 1, 0, 0) - at(f, d - 1, 0, 0)
        after = pltpu.roll(jnp.where(first_sub, at(f, d, SUBS, 0), here), SUBS - 1, 0)
        before = pltpu.roll(jnp.where(last_sub, at(f, d, -SUBS, 0), here), 1, 0)
        dx = after - before
        after = pltpu.roll(jnp.where(first_lane, at(f, d, 0, LANES), here), LANES - 1, 1)
        before = pltpu.roll(jnp.where(last_lane, at(f, d, 0, -LANES), here), 1, 1)
        dy = after - before
        total = dz * dz + dx * dx + dy * dy
        shade = 0.3 + (0.35 * jnp.abs(dz)) * lax.rsqrt(0.25 * total + 1.0)
        root = total * lax.rsqrt(jnp.maximum(total, 1e-30))
        gain = 0.25 * OPACITY_UNIT + (0.5 * OPACITY_UNIT) * root
        entry = bins_of(f)
        low = entry & (LANES - 1)
        upper = entry >= LANES
        words = [jnp.where(upper, pick(tab[f, w, 1], low), pick(tab[f, w, 0], low)) for w in range(2)]
        alpha = (words[1] >> 13).astype(jnp.float32) * gain
        lit = alpha * shade
        looked = (words[0] & (FIELD - 1), words[0] >> 13, words[1] & (FIELD - 1))
        terms = [lit * value.astype(jnp.float32) for value in looked]
        colour = terms if colour is None else [a + b for a, b in zip(colour, terms)]
        clear = 1.0 - alpha if clear is None else clear * (1.0 - alpha)
    return colour, clear


def composite(elements, backward):
    colour = through = None
    for part, clear in elements:
        if colour is None:
            colour, through = part, clear
        else:
            keep = jnp.where(backward, clear, 1.0)
            weight = jnp.where(backward, 1.0, through)
            colour = [a * keep + weight * b for a, b in zip(colour, part)]
            through = through * clear
    return colour, through


def lattice(cells, columns, depths, odd, g, start):
    _, depth, cols, _ = cells.shape
    span, here = pl.ds(g * SUBS, SUBS), pl.ds(start, LANES)

    def ghost(faces, is_odd, after, *index):
        inner, outer = (face[index] for face in faces)
        return jnp.where(is_odd != after, inner, outer)

    def at(f, d, dc, dr):
        if d < 0 or d == depth:
            return ghost(depths, odd[1], d == depth, f, 0, span, here)
        if g * SUBS + dc < 0 or g * SUBS + dc == cols:
            face = ghost(columns, odd[0], dc > 0, f, d, slice(None), here)
            return jnp.broadcast_to(face, (SUBS, LANES))
        return cells[f, d, pl.ds(g * SUBS + dc, SUBS), pl.ds(start + (LANES + dr), LANES)]

    return at


def inner_kernel(
    wide, fields, bins, xin, xout, colour, opacity, view, cells, picks, mid, tab, back, colour_now, opacity_now, view_now, field_sem, bin_sem, tab_sem
):
    depth, cols, rows = fields.shape[1:]
    groups, half = cols // SUBS, rows // 2
    small = [
        pltpu.make_async_copy(source, target, tab_sem.at[n])
        for n, (source, target) in enumerate(((colour, colour_now), (opacity, opacity_now), (view, view_now)))
    ]
    parts = (pl.ds(0, half + LANES), pl.ds(half + LANES, half - LANES))
    field_copies, bin_copies = {}, {}
    for g in range(groups):
        span = pl.ds(g * SUBS, SUBS)
        for h, part in enumerate(parts):
            target = cells.at[:, :, span, pl.ds(LANES + part.start, part.size)]
            field_copies[g, h] = pltpu.make_async_copy(fields.at[:, :, span, part], target, field_sem.at[g, h])
            part = pl.ds(h * half, half)
            bin_copies[g, h] = pltpu.make_async_copy(bins.at[:, :, span, part], picks.at[:, :, span, part], bin_sem.at[g, h])
    for copy in small:
        copy.start()
    for g in range(groups):
        for h in range(2):
            if g == 0:
                field_copies[g, h].start()
            if g + 1 < groups:
                field_copies[g + 1, h].start()
            bin_copies[g, h].start()
    zero = jnp.zeros((cols, LANES), jnp.float32)
    for f in range(2):
        for d in range(depth):
            cells[f, d, :, 0:LANES] = zero
            cells[f, d, :, LANES + rows :] = zero
    for copy in small:
        copy.wait()
    sub = lax.broadcasted_iota(jnp.int32, (SUBS, LANES), 0)
    for g in range(groups):
        towards = jnp.zeros((SUBS, LANES), jnp.int32)
        for k in range(SUBS):
            towards = jnp.where(sub == k, view_now[g * SUBS + k], towards)
        back[g * SUBS : (g + 1) * SUBS, :] = towards
    store_tables(colour_now, opacity_now, tab)
    edges = masks()
    for g in range(groups):
        backward = back[g * SUBS : (g + 1) * SUBS, :] == 1

        def tile(b, carry, g=g, backward=backward):
            start = pl.multiple_of(b * LANES, LANES)
            at = lattice(cells, (xin, xout), None, (wide[0] % 2 == 1, None), g, start)

            def element(d):
                return cell(at, lambda f: picks[f, d, pl.ds(g * SUBS, SUBS), pl.ds(start, LANES)], d, tab, edges)

            colours, through = composite((element(d) for d in range(1, depth - 1)), backward)
            for k, value in enumerate(colours + [through]):
                mid[b, k, pl.ds(g * SUBS, SUBS), :] = value
            return carry

        for h in range(2):
            if g == 0:
                field_copies[g, h].wait()
            if g + 1 < groups:
                field_copies[g + 1, h].wait()
            bin_copies[g, h].wait()
            lax.fori_loop(h * half // LANES, (h + 1) * half // LANES, tile, 0, unroll=4)


def outer_kernel(wide, narrow, cells, zin, zout, xin, xout, picks, mid, tab, back, out):
    depth, cols, rows = picks.shape[1:]
    edges = masks()
    for g in range(cols // SUBS):
        backward = back[g * SUBS : (g + 1) * SUBS, :] == 1

        def tile(b, carry, g=g, backward=backward):
            start = pl.multiple_of(b * LANES, LANES)
            at = lattice(cells, (xin, xout), (zin, zout), (wide[0] % 2 == 1, narrow[0] % 2 == 1), g, start)

            def element(d):
                return cell(at, lambda f: picks[f, d, pl.ds(g * SUBS, SUBS), pl.ds(start, LANES)], d, tab, edges)

            middle = [mid[b, k, pl.ds(g * SUBS, SUBS), :] for k in range(4)]
            elements = [element(0), (middle[:3], middle[3]), element(depth - 1)]
            parts, through = composite(elements, backward)
            for k, part in enumerate(parts):
                out[b, k, pl.ds(g * SUBS, SUBS), :] = part * COLOUR_UNIT
            out[b, 3, pl.ds(g * SUBS, SUBS), :] = 1.0 - through
            return carry

        lax.fori_loop(0, rows // LANES, tile, 0, unroll=8)


VMEM = pl.BlockSpec(memory_space=pltpu.VMEM)
SMEM = pl.BlockSpec(memory_space=pltpu.SMEM)
ANY = pl.BlockSpec(memory_space=pl.ANY)
LIMIT = 24 * 2**20


def march_inner(wide, fields, bins, xin, xout, colour, opacity, view):
    _, depth, cols, rows = fields.shape
    resident = [pltpu.with_memory_space_constraint(x, pltpu.HBM) for x in (fields, bins)]
    tables = [pltpu.with_memory_space_constraint(x, pltpu.HBM) for x in (colour, opacity, view)]
    return pl.pallas_call(
        inner_kernel,
        out_shape=[
            pltpu.VMEM((2, depth, cols, rows + 2 * LANES), jnp.float32),
            pltpu.VMEM((2, depth, cols, rows), jnp.int32),
            pltpu.VMEM((rows // LANES, 4, cols, LANES), jnp.float32),
            pltpu.VMEM((2, 2, 2, SUBS, LANES), jnp.int32),
            pltpu.VMEM((cols, LANES), jnp.int32),
        ],
        in_specs=[SMEM, ANY, ANY, VMEM, VMEM, ANY, ANY, ANY],
        out_specs=[VMEM] * 5,
        scratch_shapes=[
            pltpu.VMEM(colour.shape, colour.dtype),
            pltpu.VMEM(opacity.shape, opacity.dtype),
            pltpu.SMEM(view.shape, view.dtype),
            pltpu.SemaphoreType.DMA((cols // SUBS, 2)),
            pltpu.SemaphoreType.DMA((cols // SUBS, 2)),
            pltpu.SemaphoreType.DMA((3,)),
        ],
        compiler_params=pltpu.CompilerParams(vmem_limit_bytes=LIMIT),
        cost_estimate=pl.CostEstimate(flops=50_000 * 2 * depth * cols * rows, bytes_accessed=64 * 2**20, transcendentals=0),
        name="march_inner",
    )(wide, *resident, xin, xout, *tables)


def march_outer(wide, narrow, cells, zin, zout, xin, xout, picks, mid, tab, back):
    _, depth, cols, rows = picks.shape
    return pl.pallas_call(
        outer_kernel,
        out_shape=pltpu.VMEM((rows // LANES, 4, cols, LANES), jnp.float32),
        in_specs=[SMEM] * 2 + [VMEM] * 9,
        out_specs=VMEM,
        compiler_params=pltpu.CompilerParams(vmem_limit_bytes=LIMIT),
        name="march_outer",
    )(wide, narrow, cells, zin, zout, xin, xout, picks, mid, tab, back)


def join_kernel(parts, back, out):
    depth, _, cols, _ = parts.shape
    for group in range(cols // SUBS):
        span = pl.ds(group * SUBS, SUBS)
        elements = (([parts[d, k, span, :] for k in range(3)], 1.0 - parts[d, 3, span, :]) for d in range(depth))
        colour, through = composite(elements, back[span, :] == 1)
        for k in range(3):
            out[k, span, :] = colour[k]
        out[3, span, :] = 1.0 - through


def join(parts, back):
    return pl.pallas_call(
        join_kernel,
        out_shape=pltpu.VMEM(parts.shape[1:], jnp.float32),
        in_specs=[VMEM, VMEM],
        out_specs=VMEM,
        name="join",
    )(pltpu.with_memory_space_constraint(parts, pltpu.VMEM), back)


Z, X, CORES = 8, 4, 2
PIECES = 4


def device(z, x, core):
    return (z % Z * X + x % X) * CORES + core


def everywhere(target):
    places = [(z, x, core) for z in range(Z) for x in range(X) for core in range(CORES)]
    return [(device(*spot), device(*target(*spot))) for spot in places]


def pairs(partner):
    return [list(pair) for pair in everywhere(partner) if pair[0] < pair[1]]


DOUBLINGS = (
    pairs(lambda z, x, core: (z ^ 4, x, core)),
    pairs(lambda z, x, core: (z, x ^ 2, core) if core else (z ^ 2, x, core)),
    pairs(lambda z, x, core: (z, x ^ 1, core) if core else (z ^ 1, x, core)),
)


def beside(place):
    return place + 1 if place % 2 else place - 1


MOVES = (
    everywhere(lambda z, x, core: (z ^ 1, x, core) if core else (z, x ^ 1, core)),
    everywhere(lambda z, x, core: (beside(z), x, core) if core else (z, beside(x), core)),
    everywhere(lambda z, x, core: (z - 2 if z % 2 else z + 2, x, core) if core else (z, x + 2, core)),
)
SWAP = everywhere(lambda z, x, core: (z, x, 1 - core))


def gather(block):
    for groups in DOUBLINGS:
        block = lax.all_gather(block, "wide", axis_index_groups=groups)
    return [block] + [lax.ppermute(block, "wide", move) for move in MOVES]


def place_kernel(swapped, spot, *refs):
    pieces, out, sem = refs[:PIECES], refs[-2], refs[-1]
    wide = spot[0]
    core = (wide + swapped) % CORES
    x, z = wide // CORES % X, wide // (CORES * X)
    copies = []
    for piece in range(PIECES):
        steps = (0, 1 - 2 * (z % 2), 2 * (z % 2) - 1, 2), (0, 1 - 2 * (x % 2), 2 * (x % 2) - 1, 2)
        z_from, x_from = (z + Z + steps[0][piece]) % (Z // 2), (x + X + steps[1][piece]) % X
        for third in range(2):
            for second in range(2):
                for first in range(2):
                    z_now = jnp.where(core == 0, 4 * first + 2 * second + third, 4 * first + z_from)
                    x_now = jnp.where(core == 0, x_from, 2 * second + third)
                    target = out.at[:, z_now, x_now, core]
                    copies.append(pltpu.make_async_copy(pieces[piece].at[third, second, first], target, sem))
    for copy in copies:
        copy.start()
    for copy in copies:
        copy.wait()


def place(pieces, spot, swapped, frame=None):
    channels, cols, rows = pieces[0].shape[3:]
    kept = [] if frame is None else [frame]
    return pl.pallas_call(
        functools.partial(place_kernel, swapped),
        in_specs=[SMEM] + [VMEM] * PIECES + [ANY] * len(kept),
        out_specs=ANY,
        out_shape=jax.ShapeDtypeStruct((channels, Z, X, CORES, cols, rows), jnp.float32),
        scratch_shapes=[pltpu.SemaphoreType.DMA],
        input_output_aliases={1 + PIECES: 0} if kept else {},
        compiler_params=pltpu.CompilerParams(vmem_limit_bytes=2**20),
        cost_estimate=pl.CostEstimate(flops=0, bytes_accessed=4 * 2**20, transcendentals=0),
        name="place",
    )(spot, *(pltpu.with_memory_space_constraint(piece, pltpu.VMEM) for piece in pieces), *kept)


def faces(low, high, axis):
    odd = lax.axis_index(axis) & 1 == 1
    return jnp.where(odd, low, high), jnp.where(odd, high, low)


def change(inner, outer, axis):
    count = lax.axis_size(axis)
    route = [(i, beside(i)) for i in range(count) if 0 <= beside(i) < count]
    return lax.ppermute(inner, axis, [(i, i ^ 1) for i in range(count)]), lax.ppermute(outer, axis, route)


def on_device(fields, field_bins, colour_table, opacity_table, view_dir):
    depth, cols = fields.shape[1:3]
    wide, narrow = (lax.axis_index(axis).reshape(1) for axis in ("wide", "narrow"))
    *columns, fields_after = lax.optimization_barrier((*faces(fields[:, :, :1], fields[:, :, cols - 1 :], "wide"), fields))
    xin, xout = change(*columns, "wide")
    zin, zout = change(*faces(fields_after[:, :1], fields_after[:, depth - 1 :], "narrow"), "narrow")
    colour = jnp.transpose(colour_table, (1, 0, 2))
    cells, picks, mid, tab, back = march_inner(wide, fields, field_bins, xin, xout, colour, opacity_table, view_dir)
    partial = march_outer(wide, narrow, cells, zin, zout, xin, xout, picks, mid, tab, back)
    partial = lax.all_to_all(partial, "narrow", 0, 0)
    own = gather(join(partial, back))
    other = [lax.ppermute(piece, "wide", SWAP) for piece in own]
    frame = place(other, wide, 1, place(own, wide, 0))
    return frame.reshape(frame.shape[0], -1, frame.shape[-1])


def solution(mesh):
    split = P(None, "narrow", "wide", None)
    return jax.shard_map(
        on_device,
        mesh=mesh,
        in_specs=(split, split, P(), P(), P("wide")),
        out_specs=P(None, None, "narrow"),
        check_vma=False,
    )
```

```python
import functools

import jax
import jax.numpy as jnp
from jax import lax
from jax.experimental import pallas as pl
from jax.experimental.pallas import tpu as pltpu
from jax.sharding import PartitionSpec as P

LANES = 128
SUBS = 8
COLOUR_UNIT = 2.0**-12
OPACITY_UNIT = 2.0**-18
FIELD = 1 << 13

LOOKUP = lax.GatherDimensionNumbers(
    offset_dims=(),
    collapsed_slice_dims=(1,),
    start_index_map=(1,),
    operand_batching_dims=(0,),
    start_indices_batching_dims=(0,),
)


def pick(table, lanes):
    return lax.gather(table, lanes[..., None], LOOKUP, (1, 1), mode=lax.GatherScatterMode.PROMISE_IN_BOUNDS)


def store_tables(colour_ref, opacity_ref, tab):
    for f in range(2):
        colour = [(colour_ref[k, f : f + 1, :].astype(jnp.float32) / COLOUR_UNIT).astype(jnp.int32) for k in range(3)]
        opacity = (opacity_ref[f : f + 1, :].astype(jnp.float32) / OPACITY_UNIT).astype(jnp.int32)
        for w, word in enumerate((colour[0] + colour[1] * FIELD, colour[2] + opacity * FIELD)):
            for h in range(2):
                tab[f, w, h] = jnp.broadcast_to(word[:, h * LANES : (h + 1) * LANES], (SUBS, LANES))


def masks():
    sub = lax.broadcasted_iota(jnp.int32, (SUBS, LANES), 0)
    lane = lax.broadcasted_iota(jnp.int32, (SUBS, LANES), 1)
    return sub == 0, sub == SUBS - 1, lane == 0, lane == LANES - 1


def cell(at, bins_of, d, tab, edges):
    first_sub, last_sub, first_lane, last_lane = edges
    colour = clear = None
    for f in range(2):
        here = at(f, d, 0, 0)
        dz = at(f, d + 1, 0, 0) - at(f, d - 1, 0, 0)
        after = pltpu.roll(jnp.where(first_sub, at(f, d, SUBS, 0), here), SUBS - 1, 0)
        before = pltpu.roll(jnp.where(last_sub, at(f, d, -SUBS, 0), here), 1, 0)
        dx = after - before
        after = pltpu.roll(jnp.where(first_lane, at(f, d, 0, LANES), here), LANES - 1, 1)
        before = pltpu.roll(jnp.where(last_lane, at(f, d, 0, -LANES), here), 1, 1)
        dy = after - before
        total = dz * dz + dx * dx + dy * dy
        shade = 0.3 + (0.35 * jnp.abs(dz)) * lax.rsqrt(0.25 * total + 1.0)
        root = total * lax.rsqrt(jnp.maximum(total, 1e-30))
        gain = 0.25 * OPACITY_UNIT + (0.5 * OPACITY_UNIT) * root
        entry = bins_of(f)
        low = entry & (LANES - 1)
        upper = entry >= LANES
        words = [jnp.where(upper, pick(tab[f, w, 1], low), pick(tab[f, w, 0], low)) for w in range(2)]
        alpha = (words[1] >> 13).astype(jnp.float32) * gain
        lit = alpha * shade
        looked = (words[0] & (FIELD - 1), words[0] >> 13, words[1] & (FIELD - 1))
        terms = [lit * value.astype(jnp.float32) for value in looked]
        colour = terms if colour is None else [a + b for a, b in zip(colour, terms)]
        clear = 1.0 - alpha if clear is None else clear * (1.0 - alpha)
    return colour, clear


def composite(elements, backward):
    colour = through = None
    for part, clear in elements:
        if colour is None:
            colour, through = part, clear
        else:
            keep = jnp.where(backward, clear, 1.0)
            weight = jnp.where(backward, 1.0, through)
            colour = [a * keep + weight * b for a, b in zip(colour, part)]
            through = through * clear
    return colour, through


def lattice(cells, columns, depths, odd, g, start):
    _, depth, cols, _ = cells.shape
    span, here = pl.ds(g * SUBS, SUBS), pl.ds(start, LANES)

    def ghost(faces, is_odd, after, *index):
        inner, outer = (face[index] for face in faces)
        return jnp.where(is_odd != after, inner, outer)

    def at(f, d, dc, dr):
        if d < 0 or d == depth:
            return ghost(depths, odd[1], d == depth, f, 0, span, here)
        if g * SUBS + dc < 0 or g * SUBS + dc == cols:
            face = ghost(columns, odd[0], dc > 0, f, d, slice(None), here)
            return jnp.broadcast_to(face, (SUBS, LANES))
        return cells[f, d, pl.ds(g * SUBS + dc, SUBS), pl.ds(start + (LANES + dr), LANES)]

    return at


def load_kernel(
    wide, narrow, fields, colour, opacity, view, cells, xin, xout, zin, zout, tab, back, colour_now, opacity_now, view_now, field_sem, tab_sem
):
    depth, cols, rows = fields.shape[1:]
    small = [
        pltpu.make_async_copy(source, target, tab_sem.at[n])
        for n, (source, target) in enumerate(((colour, colour_now), (opacity, opacity_now), (view, view_now)))
    ]
    for copy in small:
        copy.start()
    ends = (0, depth - 1)
    order = ends + tuple(range(1, depth - 1))
    copies = {}
    for d in order:
        copies[d] = pltpu.make_async_copy(fields.at[:, d], cells.at[:, d, :, pl.ds(LANES, rows)], field_sem.at[d])
        copies[d].start()
    zero = jnp.zeros((cols, LANES), jnp.float32)
    for f in range(2):
        for d in range(depth):
            cells[f, d, :, 0:LANES] = zero
            cells[f, d, :, LANES + rows :] = zero
    for copy in small:
        copy.wait()
    sub = lax.broadcasted_iota(jnp.int32, (SUBS, LANES), 0)
    for g in range(cols // SUBS):
        towards = jnp.zeros((SUBS, LANES), jnp.int32)
        for k in range(SUBS):
            towards = jnp.where(sub == k, view_now[g * SUBS + k], towards)
        back[g * SUBS : (g + 1) * SUBS, :] = towards
    store_tables(colour_now, opacity_now, tab)
    x_odd, z_odd = wide[0] % 2 == 1, narrow[0] % 2 == 1
    inside = slice(LANES, LANES + rows)
    for n, d in enumerate(order):
        copies[d].wait()
        for f in range(2):
            low, high = cells[f, d, 0:1, inside], cells[f, d, cols - 1 : cols, inside]
            xin[f, d] = jnp.where(x_odd, low, high)
            xout[f, d] = jnp.where(x_odd, high, low)
            if n == 1:
                low, high = (cells[f, end, :, inside] for end in ends)
                zin[f, 0] = jnp.where(z_odd, low, high)
                zout[f, 0] = jnp.where(z_odd, high, low)


def inner_kernel(bins, cells, tab, back, picks, mid, bin_sem):
    depth, cols, rows = bins.shape[1:]
    groups, half = cols // SUBS, rows // 2
    bin_copies = {}
    inner = range(1, groups - 1)
    for g in (*inner, 0, groups - 1):
        for h in range(2):
            part = pl.ds(g * SUBS, SUBS), pl.ds(h * half, half)
            bin_copies[g, h] = pltpu.make_async_copy(bins.at[:, :, *part], picks.at[:, :, *part], bin_sem.at[g, h])
            bin_copies[g, h].start()
    edges = masks()
    for g in inner:
        backward = back[g * SUBS : (g + 1) * SUBS, :] == 1

        def tile(b, carry, g=g, backward=backward):
            start = pl.multiple_of(b * LANES, LANES)
            at = lattice(cells, None, None, None, g, start)

            def element(d):
                return cell(at, lambda f: picks[f, d, pl.ds(g * SUBS, SUBS), pl.ds(start, LANES)], d, tab, edges)

            colours, through = composite((element(d) for d in range(1, depth - 1)), backward)
            for k, value in enumerate(colours + [through]):
                mid[b, k, pl.ds((g - 1) * SUBS, SUBS), :] = value
            return carry

        for h in range(2):
            bin_copies[g, h].wait()
            lax.fori_loop(h * half // LANES, (h + 1) * half // LANES, tile, 0, unroll=4)
    for g in (0, groups - 1):
        for h in range(2):
            bin_copies[g, h].wait()


def outer_kernel(wide, narrow, cells, zin, zout, xin, xout, picks, mid, tab, back, out):
    depth, cols, rows = picks.shape[1:]
    groups = cols // SUBS
    edges = masks()
    odd = wide[0] % 2 == 1, narrow[0] % 2 == 1
    for g in range(groups):
        backward = back[g * SUBS : (g + 1) * SUBS, :] == 1
        inside = 0 < g < groups - 1

        def tile(b, carry, g=g, backward=backward, inside=inside):
            start = pl.multiple_of(b * LANES, LANES)
            at = lattice(cells, (xin, xout), (zin, zout), odd, g, start)

            def element(d):
                return cell(at, lambda f: picks[f, d, pl.ds(g * SUBS, SUBS), pl.ds(start, LANES)], d, tab, edges)

            if inside:
                middle = [mid[b, k, pl.ds((g - 1) * SUBS, SUBS), :] for k in range(4)]
                elements = [element(0), (middle[:3], middle[3]), element(depth - 1)]
            else:
                elements = (element(d) for d in range(depth))
            colours, through = composite(elements, backward)
            for k, value in enumerate(colours):
                out[b, k, pl.ds(g * SUBS, SUBS), :] = value * COLOUR_UNIT
            out[b, 3, pl.ds(g * SUBS, SUBS), :] = 1.0 - through
            return carry

        lax.fori_loop(0, rows // LANES, tile, 0, unroll=8 if inside else 4)


VMEM = pl.BlockSpec(memory_space=pltpu.VMEM)
SMEM = pl.BlockSpec(memory_space=pltpu.SMEM)
ANY = pl.BlockSpec(memory_space=pl.ANY)
LIMIT = 24 * 2**20


def load(wide, narrow, fields, colour, opacity, view):
    _, depth, cols, rows = fields.shape
    fields, colour, opacity, view = (pltpu.with_memory_space_constraint(x, pltpu.HBM) for x in (fields, colour, opacity, view))
    return pl.pallas_call(
        load_kernel,
        out_shape=[
            pltpu.VMEM((2, depth, cols, rows + 2 * LANES), jnp.float32),
            pltpu.VMEM((2, depth, 1, rows), jnp.float32),
            pltpu.VMEM((2, depth, 1, rows), jnp.float32),
            pltpu.VMEM((2, 1, cols, rows), jnp.float32),
            pltpu.VMEM((2, 1, cols, rows), jnp.float32),
            pltpu.VMEM((2, 2, 2, SUBS, LANES), jnp.int32),
            pltpu.VMEM((cols, LANES), jnp.int32),
        ],
        in_specs=[SMEM, SMEM, ANY, ANY, ANY, ANY],
        out_specs=[VMEM] * 7,
        scratch_shapes=[
            pltpu.VMEM(colour.shape, colour.dtype),
            pltpu.VMEM(opacity.shape, opacity.dtype),
            pltpu.SMEM(view.shape, view.dtype),
            pltpu.SemaphoreType.DMA((depth,)),
            pltpu.SemaphoreType.DMA((3,)),
        ],
        compiler_params=pltpu.CompilerParams(vmem_limit_bytes=LIMIT),
        name="load",
    )(wide, narrow, fields, colour, opacity, view)


def march_inner(bins, cells, tab, back):
    _, depth, cols, rows = bins.shape
    return pl.pallas_call(
        inner_kernel,
        out_shape=[
            pltpu.VMEM((2, depth, cols, rows), jnp.int32),
            pltpu.VMEM((rows // LANES, 4, cols - 2 * SUBS, LANES), jnp.float32),
        ],
        in_specs=[ANY, VMEM, VMEM, VMEM],
        out_specs=[VMEM] * 2,
        scratch_shapes=[pltpu.SemaphoreType.DMA((cols // SUBS, 2))],
        compiler_params=pltpu.CompilerParams(vmem_limit_bytes=LIMIT),
        cost_estimate=pl.CostEstimate(flops=100 * 2 * depth * cols * rows, bytes_accessed=8 * 2**20, transcendentals=0),
        name="march_inner",
    )(pltpu.with_memory_space_constraint(bins, pltpu.HBM), cells, tab, back)


def march_outer(wide, narrow, cells, zin, zout, xin, xout, picks, mid, tab, back):
    _, depth, cols, rows = picks.shape
    return pl.pallas_call(
        outer_kernel,
        out_shape=pltpu.VMEM((rows // LANES, 4, cols, LANES), jnp.float32),
        in_specs=[SMEM] * 2 + [VMEM] * 9,
        out_specs=VMEM,
        compiler_params=pltpu.CompilerParams(vmem_limit_bytes=LIMIT),
        name="march_outer",
    )(wide, narrow, cells, zin, zout, xin, xout, picks, mid, tab, back)


def join_kernel(parts, back, out):
    depth, _, cols, _ = parts.shape
    for group in range(cols // SUBS):
        span = pl.ds(group * SUBS, SUBS)
        elements = (([parts[d, k, span, :] for k in range(3)], 1.0 - parts[d, 3, span, :]) for d in range(depth))
        colour, through = composite(elements, back[span, :] == 1)
        for k in range(3):
            out[k, span, :] = colour[k]
        out[3, span, :] = 1.0 - through


def join(parts, back):
    return pl.pallas_call(
        join_kernel,
        out_shape=pltpu.VMEM(parts.shape[1:], jnp.float32),
        in_specs=[VMEM, VMEM],
        out_specs=VMEM,
        name="join",
    )(pltpu.with_memory_space_constraint(parts, pltpu.VMEM), back)


Z, X, CORES = 8, 4, 2
PIECES = 4


def device(z, x, core):
    return (z % Z * X + x % X) * CORES + core


def everywhere(target):
    places = [(z, x, core) for z in range(Z) for x in range(X) for core in range(CORES)]
    return [(device(*spot), device(*target(*spot))) for spot in places]


def pairs(partner):
    return [list(pair) for pair in everywhere(partner) if pair[0] < pair[1]]


DOUBLINGS = (
    pairs(lambda z, x, core: (z ^ 4, x, core)),
    pairs(lambda z, x, core: (z, x ^ 2, core) if core else (z ^ 2, x, core)),
    pairs(lambda z, x, core: (z, x ^ 1, core) if core else (z ^ 1, x, core)),
)


def beside(place):
    return place + 1 if place % 2 else place - 1


MOVES = (
    everywhere(lambda z, x, core: (z ^ 1, x, core) if core else (z, x ^ 1, core)),
    everywhere(lambda z, x, core: (beside(z), x, core) if core else (z, beside(x), core)),
    everywhere(lambda z, x, core: (z - 2 if z % 2 else z + 2, x, core) if core else (z, x + 2, core)),
)
SWAP = everywhere(lambda z, x, core: (z, x, 1 - core))


def gather(block):
    for groups in DOUBLINGS:
        block = lax.all_gather(block, "wide", axis_index_groups=groups)
    return [block] + [lax.ppermute(block, "wide", move) for move in MOVES]


def place_kernel(swapped, spot, *refs):
    pieces, out, sem = refs[:PIECES], refs[-2], refs[-1]
    wide = spot[0]
    core = (wide + swapped) % CORES
    x, z = wide // CORES % X, wide // (CORES * X)
    copies = []
    for piece in range(PIECES):
        steps = (0, 1 - 2 * (z % 2), 2 * (z % 2) - 1, 2), (0, 1 - 2 * (x % 2), 2 * (x % 2) - 1, 2)
        z_from, x_from = (z + Z + steps[0][piece]) % (Z // 2), (x + X + steps[1][piece]) % X
        for third in range(2):
            for second in range(2):
                for first in range(2):
                    z_now = jnp.where(core == 0, 4 * first + 2 * second + third, 4 * first + z_from)
                    x_now = jnp.where(core == 0, x_from, 2 * second + third)
                    target = out.at[:, z_now, x_now, core]
                    copies.append(pltpu.make_async_copy(pieces[piece].at[third, second, first], target, sem))
    for copy in copies:
        copy.start()
    for copy in copies:
        copy.wait()


def place(pieces, spot, swapped, frame=None):
    channels, cols, rows = pieces[0].shape[3:]
    kept = [] if frame is None else [frame]
    return pl.pallas_call(
        functools.partial(place_kernel, swapped),
        in_specs=[SMEM] + [VMEM] * PIECES + [ANY] * len(kept),
        out_specs=ANY,
        out_shape=jax.ShapeDtypeStruct((channels, Z, X, CORES, cols, rows), jnp.float32),
        scratch_shapes=[pltpu.SemaphoreType.DMA],
        input_output_aliases={1 + PIECES: 0} if kept else {},
        compiler_params=pltpu.CompilerParams(vmem_limit_bytes=2**20),
        cost_estimate=pl.CostEstimate(flops=0, bytes_accessed=4 * 2**20, transcendentals=0),
        name="place",
    )(spot, *(pltpu.with_memory_space_constraint(piece, pltpu.VMEM) for piece in pieces), *kept)


def change(inner, outer, axis):
    count = lax.axis_size(axis)
    route = [(i, beside(i)) for i in range(count) if 0 <= beside(i) < count]
    return lax.ppermute(inner, axis, [(i, i ^ 1) for i in range(count)]), lax.ppermute(outer, axis, route)


def on_device(fields, field_bins, colour_table, opacity_table, view_dir):
    wide, narrow = (lax.axis_index(axis).reshape(1) for axis in ("wide", "narrow"))
    colour = jnp.transpose(colour_table, (1, 0, 2))
    cells, *faces, tab, back = load(wide, narrow, fields, colour, opacity_table, view_dir)
    zin, zout = change(*faces[2:], "narrow")
    xin, xout = change(*faces[:2], "wide")
    picks, mid = march_inner(field_bins, cells, tab, back)
    partial = march_outer(wide, narrow, cells, zin, zout, xin, xout, picks, mid, tab, back)
    partial = lax.all_to_all(partial, "narrow", 0, 0)
    own = gather(join(partial, back))
    other = [lax.ppermute(piece, "wide", SWAP) for piece in own]
    frame = place(other, wide, 1, place(own, wide, 0))
    return frame.reshape(frame.shape[0], -1, frame.shape[-1])


def solution(mesh):
    split = P(None, "narrow", "wide", None)
    return jax.shard_map(
        on_device,
        mesh=mesh,
        in_specs=(split, split, P(), P(), P("wide")),
        out_specs=P(None, None, "narrow"),
        check_vma=False,
    )
```

```python
import functools

import jax
import jax.numpy as jnp
from jax import lax
from jax.experimental import pallas as pl
from jax.experimental.pallas import tpu as pltpu
from jax.sharding import PartitionSpec as P

LANES = 128
SUBS = 8
COLOUR_UNIT = 2.0**-12
OPACITY_UNIT = 2.0**-18
FIELD = 1 << 13

LOOKUP = lax.GatherDimensionNumbers(
    offset_dims=(),
    collapsed_slice_dims=(1,),
    start_index_map=(1,),
    operand_batching_dims=(0,),
    start_indices_batching_dims=(0,),
)


def pick(table, lanes):
    return lax.gather(table, lanes[..., None], LOOKUP, (1, 1), mode=lax.GatherScatterMode.PROMISE_IN_BOUNDS)


def store_tables(colour_ref, opacity_ref, tab):
    for f in range(2):
        colour = [(colour_ref[k, f : f + 1, :].astype(jnp.float32) / COLOUR_UNIT).astype(jnp.int32) for k in range(3)]
        opacity = (opacity_ref[f : f + 1, :].astype(jnp.float32) / OPACITY_UNIT).astype(jnp.int32)
        for w, word in enumerate((colour[0] + colour[1] * FIELD, colour[2] + opacity * FIELD)):
            for h in range(2):
                tab[f, w, h] = jnp.broadcast_to(word[:, h * LANES : (h + 1) * LANES], (SUBS, LANES))


def ends(axis, length):
    place = lax.broadcasted_iota(jnp.int32, (SUBS, LANES), axis)
    return place == 0, place == length - 1


def cell(at, slope, bins_of, d, tab, edges):
    first_sub, last_sub = edges
    colour = clear = None
    for f in range(2):
        here = at(f, d, 0)
        dz = at(f, d + 1, 0) - at(f, d - 1, 0)
        after = pltpu.roll(jnp.where(first_sub, at(f, d, SUBS), here), SUBS - 1, 0)
        before = pltpu.roll(jnp.where(last_sub, at(f, d, -SUBS), here), 1, 0)
        dx = after - before
        dy = slope(f)
        total = dz * dz + dx * dx + dy * dy
        shade = 0.3 + (0.35 * jnp.abs(dz)) * lax.rsqrt(0.25 * total + 1.0)
        root = total * lax.rsqrt(jnp.maximum(total, 1e-30))
        gain = 0.25 * OPACITY_UNIT + (0.5 * OPACITY_UNIT) * root
        entry = bins_of(f)
        low = entry & (LANES - 1)
        upper = entry >= LANES
        words = [jnp.where(upper, pick(tab[f, w, 1], low), pick(tab[f, w, 0], low)) for w in range(2)]
        alpha = (words[1] >> 13).astype(jnp.float32) * gain
        lit = alpha * shade
        looked = (words[0] & (FIELD - 1), words[0] >> 13, words[1] & (FIELD - 1))
        terms = [lit * value.astype(jnp.float32) for value in looked]
        colour = terms if colour is None else [a + b for a, b in zip(colour, terms)]
        clear = 1.0 - alpha if clear is None else clear * (1.0 - alpha)
    return colour, clear


def composite(elements, backward):
    colour = through = None
    for part, clear in elements:
        if colour is None:
            colour, through = part, clear
        else:
            keep = jnp.where(backward, clear, 1.0)
            weight = jnp.where(backward, 1.0, through)
            colour = [a * keep + weight * b for a, b in zip(colour, part)]
            through = through * clear
    return colour, through


def lattice(cells, columns, depths, odd, g, start):
    _, depth, cols, _ = cells.shape
    span, here = pl.ds(g * SUBS, SUBS), pl.ds(start, LANES)

    def ghost(faces, is_odd, after, *index):
        inner, outer = (face[index] for face in faces)
        return jnp.where(is_odd != after, inner, outer)

    def at(f, d, dc):
        if d < 0 or d == depth:
            return ghost(depths, odd[1], d == depth, f, 0, span, here)
        if g * SUBS + dc < 0 or g * SUBS + dc == cols:
            face = ghost(columns, odd[0], dc > 0, f, d, slice(None), here)
            return jnp.broadcast_to(face, (SUBS, LANES))
        return cells[f, d, pl.ds(g * SUBS + dc, SUBS), here]

    return at


def load_kernel(
    wide, narrow, fields, colour, opacity, view, cells, xin, xout, zin, zout, tab, back, colour_now, opacity_now, view_now, field_sem, tab_sem
):
    depth, cols, rows = fields.shape[1:]
    small = [
        pltpu.make_async_copy(source, target, tab_sem.at[n])
        for n, (source, target) in enumerate(((colour, colour_now), (opacity, opacity_now), (view, view_now)))
    ]
    for copy in small:
        copy.start()
    sides = (0, depth - 1)
    order = sides + tuple(range(1, depth - 1))
    copies = {}
    for d in order:
        copies[d] = pltpu.make_async_copy(fields.at[:, d], cells.at[:, d], field_sem.at[d])
        copies[d].start()
    for copy in small:
        copy.wait()
    sub = lax.broadcasted_iota(jnp.int32, (SUBS, LANES), 0)
    for g in range(cols // SUBS):
        towards = jnp.zeros((SUBS, LANES), jnp.int32)
        for k in range(SUBS):
            towards = jnp.where(sub == k, view_now[g * SUBS + k], towards)
        back[g * SUBS : (g + 1) * SUBS, :] = towards
    store_tables(colour_now, opacity_now, tab)
    x_odd, z_odd = wide[0] % 2 == 1, narrow[0] % 2 == 1
    for n, d in enumerate(order):
        copies[d].wait()
        for f in range(2):
            low, high = cells[f, d, 0:1, :], cells[f, d, cols - 1 : cols, :]
            xin[f, d] = jnp.where(x_odd, low, high)
            xout[f, d] = jnp.where(x_odd, high, low)
            if n == 1:
                low, high = (cells[f, end] for end in sides)
                zin[f, 0] = jnp.where(z_odd, low, high)
                zout[f, 0] = jnp.where(z_odd, high, low)


def inner_kernel(bins, cells, tab, back, picks, slopes, mid, bin_sem):
    depth, cols, rows = bins.shape[1:]
    groups, half = cols // SUBS, rows // 2
    bin_copies = {}
    inner = range(1, groups - 1)
    for g in (*inner, 0, groups - 1):
        for h in range(2):
            part = pl.ds(g * SUBS, SUBS), pl.ds(h * half, half)
            bin_copies[g, h] = pltpu.make_async_copy(bins.at[:, :, *part], picks.at[:, :, *part], bin_sem.at[g, h])
            bin_copies[g, h].start()
    first_lane, last_lane = ends(1, LANES)
    zero = jnp.zeros((SUBS, LANES), jnp.float32)

    def differ(step, carry):
        d, span = step // groups, pl.ds(pl.multiple_of(step % groups * SUBS, SUBS), SUBS)
        for f in range(2):
            tiles = [zero] + [cells[f, d, span, b * LANES : (b + 1) * LANES] for b in range(rows // LANES)] + [zero]
            for b in range(rows // LANES):
                before, here, after = tiles[b : b + 3]
                after = pltpu.roll(jnp.where(first_lane, after, here), LANES - 1, 1)
                before = pltpu.roll(jnp.where(last_lane, before, here), 1, 1)
                slopes[f, d, span, b * LANES : (b + 1) * LANES] = after - before
        return carry

    lax.fori_loop(0, depth * groups, differ, 0, unroll=4)
    edges = ends(0, SUBS)
    for g in inner:
        backward = back[g * SUBS : (g + 1) * SUBS, :] == 1

        def tile(b, carry, g=g, backward=backward):
            start = pl.multiple_of(b * LANES, LANES)
            at = lattice(cells, None, None, None, g, start)

            def element(d):
                here = pl.ds(g * SUBS, SUBS), pl.ds(start, LANES)
                return cell(at, lambda f: slopes[f, d, *here], lambda f: picks[f, d, *here], d, tab, edges)

            colours, through = composite((element(d) for d in range(1, depth - 1)), backward)
            for k, value in enumerate(colours + [through]):
                mid[b, k, pl.ds((g - 1) * SUBS, SUBS), :] = value
            return carry

        for h in range(2):
            bin_copies[g, h].wait()
            lax.fori_loop(h * half // LANES, (h + 1) * half // LANES, tile, 0, unroll=4)
    for g in (0, groups - 1):
        for h in range(2):
            bin_copies[g, h].wait()


def outer_kernel(wide, narrow, cells, slopes, zin, zout, xin, xout, picks, mid, tab, back, out):
    depth, cols, rows = picks.shape[1:]
    groups = cols // SUBS
    edges = ends(0, SUBS)
    odd = wide[0] % 2 == 1, narrow[0] % 2 == 1
    for g in range(groups):
        backward = back[g * SUBS : (g + 1) * SUBS, :] == 1
        inside = 0 < g < groups - 1

        def tile(b, carry, g=g, backward=backward, inside=inside):
            start = pl.multiple_of(b * LANES, LANES)
            at = lattice(cells, (xin, xout), (zin, zout), odd, g, start)

            def element(d):
                here = pl.ds(g * SUBS, SUBS), pl.ds(start, LANES)
                return cell(at, lambda f: slopes[f, d, *here], lambda f: picks[f, d, *here], d, tab, edges)

            if inside:
                middle = [mid[b, k, pl.ds((g - 1) * SUBS, SUBS), :] for k in range(4)]
                elements = [element(0), (middle[:3], middle[3]), element(depth - 1)]
            else:
                elements = (element(d) for d in range(depth))
            colours, through = composite(elements, backward)
            for k, value in enumerate(colours):
                out[b, k, pl.ds(g * SUBS, SUBS), :] = value * COLOUR_UNIT
            out[b, 3, pl.ds(g * SUBS, SUBS), :] = 1.0 - through
            return carry

        lax.fori_loop(0, rows // LANES, tile, 0, unroll=8)


VMEM = pl.BlockSpec(memory_space=pltpu.VMEM)
SMEM = pl.BlockSpec(memory_space=pltpu.SMEM)
ANY = pl.BlockSpec(memory_space=pl.ANY)
LIMIT = 24 * 2**20


def load(wide, narrow, fields, colour, opacity, view):
    _, depth, cols, rows = fields.shape
    fields, colour, opacity, view = (pltpu.with_memory_space_constraint(x, pltpu.HBM) for x in (fields, colour, opacity, view))
    return pl.pallas_call(
        load_kernel,
        out_shape=[
            pltpu.VMEM((2, depth, cols, rows), jnp.float32),
            pltpu.VMEM((2, depth, 1, rows), jnp.float32),
            pltpu.VMEM((2, depth, 1, rows), jnp.float32),
            pltpu.VMEM((2, 1, cols, rows), jnp.float32),
            pltpu.VMEM((2, 1, cols, rows), jnp.float32),
            pltpu.VMEM((2, 2, 2, SUBS, LANES), jnp.int32),
            pltpu.VMEM((cols, LANES), jnp.int32),
        ],
        in_specs=[SMEM, SMEM, ANY, ANY, ANY, ANY],
        out_specs=[VMEM] * 7,
        scratch_shapes=[
            pltpu.VMEM(colour.shape, colour.dtype),
            pltpu.VMEM(opacity.shape, opacity.dtype),
            pltpu.SMEM(view.shape, view.dtype),
            pltpu.SemaphoreType.DMA((depth,)),
            pltpu.SemaphoreType.DMA((3,)),
        ],
        compiler_params=pltpu.CompilerParams(vmem_limit_bytes=LIMIT),
        name="load",
    )(wide, narrow, fields, colour, opacity, view)


def march_inner(bins, cells, tab, back):
    _, depth, cols, rows = bins.shape
    return pl.pallas_call(
        inner_kernel,
        out_shape=[
            pltpu.VMEM((2, depth, cols, rows), jnp.int32),
            pltpu.VMEM((2, depth, cols, rows), jnp.float32),
            pltpu.VMEM((rows // LANES, 4, cols - 2 * SUBS, LANES), jnp.float32),
        ],
        in_specs=[ANY] + [VMEM] * 3,
        out_specs=[VMEM] * 3,
        scratch_shapes=[pltpu.SemaphoreType.DMA((cols // SUBS, 2))],
        compiler_params=pltpu.CompilerParams(vmem_limit_bytes=LIMIT),
        cost_estimate=pl.CostEstimate(flops=100 * 2 * depth * cols * rows, bytes_accessed=8 * 2**20, transcendentals=0),
        name="march_inner",
    )(pltpu.with_memory_space_constraint(bins, pltpu.HBM), cells, tab, back)


def march_outer(wide, narrow, cells, slopes, zin, zout, xin, xout, picks, mid, tab, back):
    _, depth, cols, rows = picks.shape
    return pl.pallas_call(
        outer_kernel,
        out_shape=pltpu.VMEM((rows // LANES, 4, cols, LANES), jnp.float32),
        in_specs=[SMEM] * 2 + [VMEM] * 10,
        out_specs=VMEM,
        compiler_params=pltpu.CompilerParams(vmem_limit_bytes=LIMIT),
        name="march_outer",
    )(wide, narrow, cells, slopes, zin, zout, xin, xout, picks, mid, tab, back)


def join_kernel(parts, back, out):
    depth, _, cols, _ = parts.shape
    for group in range(cols // SUBS):
        span = pl.ds(group * SUBS, SUBS)
        elements = (([parts[d, k, span, :] for k in range(3)], 1.0 - parts[d, 3, span, :]) for d in range(depth))
        colour, through = composite(elements, back[span, :] == 1)
        for k in range(3):
            out[k, span, :] = colour[k]
        out[3, span, :] = 1.0 - through


def join(parts, back):
    return pl.pallas_call(
        join_kernel,
        out_shape=pltpu.VMEM(parts.shape[1:], jnp.float32),
        in_specs=[VMEM, VMEM],
        out_specs=VMEM,
        name="join",
    )(pltpu.with_memory_space_constraint(parts, pltpu.VMEM), back)


Z, X, CORES = 8, 4, 2
PIECES = 4


def device(z, x, core):
    return (z % Z * X + x % X) * CORES + core


def everywhere(target):
    places = [(z, x, core) for z in range(Z) for x in range(X) for core in range(CORES)]
    return [(device(*spot), device(*target(*spot))) for spot in places]


def pairs(partner):
    return [list(pair) for pair in everywhere(partner) if pair[0] < pair[1]]


DOUBLINGS = (
    pairs(lambda z, x, core: (z ^ 4, x, core)),
    pairs(lambda z, x, core: (z, x ^ 2, core) if core else (z ^ 2, x, core)),
    pairs(lambda z, x, core: (z, x ^ 1, core) if core else (z ^ 1, x, core)),
)


def beside(place):
    return place + 1 if place % 2 else place - 1


MOVES = (
    everywhere(lambda z, x, core: (z ^ 1, x, core) if core else (z, x ^ 1, core)),
    everywhere(lambda z, x, core: (beside(z), x, core) if core else (z, beside(x), core)),
    everywhere(lambda z, x, core: (z - 2 if z % 2 else z + 2, x, core) if core else (z, x + 2, core)),
)
SWAP = everywhere(lambda z, x, core: (z, x, 1 - core))


def gather(block):
    for groups in DOUBLINGS:
        block = lax.all_gather(block, "wide", axis_index_groups=groups)
    return [block] + [lax.ppermute(block, "wide", move) for move in MOVES]


def place_kernel(swapped, spot, *refs):
    pieces, out, sem = refs[:PIECES], refs[-2], refs[-1]
    wide = spot[0]
    core = (wide + swapped) % CORES
    x, z = wide // CORES % X, wide // (CORES * X)
    copies = []
    for piece in range(PIECES):
        steps = (0, 1 - 2 * (z % 2), 2 * (z % 2) - 1, 2), (0, 1 - 2 * (x % 2), 2 * (x % 2) - 1, 2)
        z_from, x_from = (z + Z + steps[0][piece]) % (Z // 2), (x + X + steps[1][piece]) % X
        for third in range(2):
            for second in range(2):
                for first in range(2):
                    z_now = jnp.where(core == 0, 4 * first + 2 * second + third, 4 * first + z_from)
                    x_now = jnp.where(core == 0, x_from, 2 * second + third)
                    target = out.at[:, z_now, x_now, core]
                    copies.append(pltpu.make_async_copy(pieces[piece].at[third, second, first], target, sem))
    for copy in copies:
        copy.start()
    for copy in copies:
        copy.wait()


def place(pieces, spot, swapped, frame=None):
    channels, cols, rows = pieces[0].shape[3:]
    kept = [] if frame is None else [frame]
    return pl.pallas_call(
        functools.partial(place_kernel, swapped),
        in_specs=[SMEM] + [VMEM] * PIECES + [ANY] * len(kept),
        out_specs=ANY,
        out_shape=jax.ShapeDtypeStruct((channels, Z, X, CORES, cols, rows), jnp.float32),
        scratch_shapes=[pltpu.SemaphoreType.DMA],
        input_output_aliases={1 + PIECES: 0} if kept else {},
        compiler_params=pltpu.CompilerParams(vmem_limit_bytes=2**20),
        cost_estimate=pl.CostEstimate(flops=0, bytes_accessed=4 * 2**20, transcendentals=0),
        name="place",
    )(spot, *(pltpu.with_memory_space_constraint(piece, pltpu.VMEM) for piece in pieces), *kept)


def change(inner, outer, axis):
    count = lax.axis_size(axis)
    route = [(i, beside(i)) for i in range(count) if 0 <= beside(i) < count]
    return lax.ppermute(inner, axis, [(i, i ^ 1) for i in range(count)]), lax.ppermute(outer, axis, route)


def on_device(fields, field_bins, colour_table, opacity_table, view_dir):
    wide, narrow = (lax.axis_index(axis).reshape(1) for axis in ("wide", "narrow"))
    colour = jnp.transpose(colour_table, (1, 0, 2))
    cells, *faces, tab, back = load(wide, narrow, fields, colour, opacity_table, view_dir)
    zin, zout = change(*faces[2:], "narrow")
    xin, xout = change(*faces[:2], "wide")
    picks, slopes, mid = march_inner(field_bins, cells, tab, back)
    partial = march_outer(wide, narrow, cells, slopes, zin, zout, xin, xout, picks, mid, tab, back)
    partial = lax.all_to_all(partial, "narrow", 0, 0)
    own = gather(join(partial, back))
    other = [lax.ppermute(piece, "wide", SWAP) for piece in own]
    frame = place(other, wide, 1, place(own, wide, 0))
    return frame.reshape(frame.shape[0], -1, frame.shape[-1])


def solution(mesh):
    split = P(None, "narrow", "wide", None)
    return jax.shard_map(
        on_device,
        mesh=mesh,
        in_specs=(split, split, P(), P(), P("wide")),
        out_specs=P(None, None, "narrow"),
        check_vma=False,
    )
```

```python
import functools

import jax
import jax.numpy as jnp
from jax import lax
from jax.experimental import pallas as pl
from jax.experimental.pallas import tpu as pltpu
from jax.sharding import PartitionSpec as P

LANES = 128
SUBS = 8
COLOUR_UNIT = 2.0**-12
OPACITY_UNIT = 2.0**-18
FIELD = 1 << 13

LOOKUP = lax.GatherDimensionNumbers(
    offset_dims=(),
    collapsed_slice_dims=(1,),
    start_index_map=(1,),
    operand_batching_dims=(0,),
    start_indices_batching_dims=(0,),
)


def pick(table, lanes):
    return lax.gather(table, lanes[..., None], LOOKUP, (1, 1), mode=lax.GatherScatterMode.PROMISE_IN_BOUNDS)


def store_tables(colour_ref, opacity_ref, tab):
    for f in range(2):
        colour = [(colour_ref[k, f : f + 1, :].astype(jnp.float32) / COLOUR_UNIT).astype(jnp.int32) for k in range(3)]
        opacity = (opacity_ref[f : f + 1, :].astype(jnp.float32) / OPACITY_UNIT).astype(jnp.int32)
        for w, word in enumerate((colour[0] + colour[1] * FIELD, colour[2] + opacity * FIELD)):
            for h in range(2):
                tab[f, w, h] = jnp.broadcast_to(word[:, h * LANES : (h + 1) * LANES], (SUBS, LANES))


def ends(axis, length):
    place = lax.broadcasted_iota(jnp.int32, (SUBS, LANES), axis)
    return place == 0, place == length - 1


def cell(at, slope, bins_of, d, tab, edges):
    first_sub, last_sub = edges
    colour = clear = None
    for f in range(2):
        here = at(f, d, 0)
        dz = at(f, d + 1, 0) - at(f, d - 1, 0)
        after = pltpu.roll(jnp.where(first_sub, at(f, d, SUBS), here), SUBS - 1, 0)
        before = pltpu.roll(jnp.where(last_sub, at(f, d, -SUBS), here), 1, 0)
        dx = after - before
        dy = slope(f)
        total = dz * dz + dx * dx + dy * dy
        shade = 0.3 + (0.35 * jnp.abs(dz)) * lax.rsqrt(0.25 * total + 1.0)
        root = total * lax.rsqrt(jnp.maximum(total, 1e-30))
        gain = 0.25 * OPACITY_UNIT + (0.5 * OPACITY_UNIT) * root
        entry = bins_of(f)
        low = entry & (LANES - 1)
        upper = entry >= LANES
        words = [jnp.where(upper, pick(tab[f, w, 1], low), pick(tab[f, w, 0], low)) for w in range(2)]
        alpha = (words[1] >> 13).astype(jnp.float32) * gain
        lit = alpha * shade
        looked = (words[0] & (FIELD - 1), words[0] >> 13, words[1] & (FIELD - 1))
        terms = [lit * value.astype(jnp.float32) for value in looked]
        colour = terms if colour is None else [a + b for a, b in zip(colour, terms)]
        clear = 1.0 - alpha if clear is None else clear * (1.0 - alpha)
    return colour, clear


def composite(elements, backward):
    colour = through = None
    for part, clear in elements:
        if colour is None:
            colour, through = part, clear
        else:
            keep = jnp.where(backward, clear, 1.0)
            weight = jnp.where(backward, 1.0, through)
            colour = [a * keep + weight * b for a, b in zip(colour, part)]
            through = through * clear
    return colour, through


def lattice(cells, columns, depths, odd, g, start):
    _, depth, cols, _ = cells.shape
    span, here = pl.ds(g * SUBS, SUBS), pl.ds(start, LANES)

    def ghost(faces, is_odd, after, *index):
        inner, outer = (face[index] for face in faces)
        return jnp.where(is_odd != after, inner, outer)

    def at(f, d, dc):
        if d < 0 or d == depth:
            return ghost(depths, odd[1], d == depth, f, 0, span, here)
        if g * SUBS + dc < 0 or g * SUBS + dc == cols:
            face = ghost(columns, odd[0], dc > 0, f, d, slice(None), here)
            return jnp.broadcast_to(face, (SUBS, LANES))
        return cells[f, d, pl.ds(g * SUBS + dc, SUBS), here]

    return at


def load_kernel(
    wide, narrow, fields, colour, opacity, view, cells, xin, xout, zin, zout, tab, back, colour_now, opacity_now, view_now, field_sem, tab_sem
):
    depth, cols, rows = fields.shape[1:]
    small = [
        pltpu.make_async_copy(source, target, tab_sem.at[n])
        for n, (source, target) in enumerate(((colour, colour_now), (opacity, opacity_now), (view, view_now)))
    ]
    for copy in small:
        copy.start()
    sides = (0, depth - 1)
    order = sides + tuple(range(1, depth - 1))
    copies = {}
    for d in order:
        copies[d] = pltpu.make_async_copy(fields.at[:, d], cells.at[:, d], field_sem.at[d])
        copies[d].start()
    for copy in small:
        copy.wait()
    sub = lax.broadcasted_iota(jnp.int32, (SUBS, LANES), 0)
    for g in range(cols // SUBS):
        towards = jnp.zeros((SUBS, LANES), jnp.int32)
        for k in range(SUBS):
            towards = jnp.where(sub == k, view_now[g * SUBS + k], towards)
        back[g * SUBS : (g + 1) * SUBS, :] = towards
    store_tables(colour_now, opacity_now, tab)
    x_odd, z_odd = wide[0] % 2 == 1, narrow[0] % 2 == 1
    for n, d in enumerate(order):
        copies[d].wait()
        for f in range(2):
            low, high = cells[f, d, 0:1, :], cells[f, d, cols - 1 : cols, :]
            xin[f, d] = jnp.where(x_odd, low, high)
            xout[f, d] = jnp.where(x_odd, high, low)
            if n == 1:
                low, high = (cells[f, end] for end in sides)
                zin[f, 0] = jnp.where(z_odd, low, high)
                zout[f, 0] = jnp.where(z_odd, high, low)


def inner_kernel(bins, cells, tab, back, picks, slopes, mid, bin_sem):
    depth, cols, rows = bins.shape[1:]
    groups, half = cols // SUBS, rows // 2
    bin_copies = {}
    inner = range(1, groups - 1)
    for g in (*inner, 0, groups - 1):
        for h in range(2):
            part = pl.ds(g * SUBS, SUBS), pl.ds(h * half, half)
            bin_copies[g, h] = pltpu.make_async_copy(bins.at[:, :, *part], picks.at[:, :, *part], bin_sem.at[g, h])
            bin_copies[g, h].start()
    first_lane, last_lane = ends(1, LANES)
    zero = jnp.zeros((SUBS, LANES), jnp.float32)

    def differ(step, carry):
        d, span = step // groups, pl.ds(pl.multiple_of(step % groups * SUBS, SUBS), SUBS)
        for f in range(2):
            tiles = [zero] + [cells[f, d, span, b * LANES : (b + 1) * LANES] for b in range(rows // LANES)] + [zero]
            for b in range(rows // LANES):
                before, here, after = tiles[b : b + 3]
                after = pltpu.roll(jnp.where(first_lane, after, here), LANES - 1, 1)
                before = pltpu.roll(jnp.where(last_lane, before, here), 1, 1)
                slopes[f, d, span, b * LANES : (b + 1) * LANES] = after - before
        return carry

    lax.fori_loop(0, depth * groups, differ, 0, unroll=4)
    edges = ends(0, SUBS)
    for g in inner:
        backward = back[g * SUBS : (g + 1) * SUBS, :] == 1

        def tile(b, carry, g=g, backward=backward):
            start = pl.multiple_of(b * LANES, LANES)
            at = lattice(cells, None, None, None, g, start)

            def element(d):
                here = pl.ds(g * SUBS, SUBS), pl.ds(start, LANES)
                return cell(at, lambda f: slopes[f, d, *here], lambda f: picks[f, d, *here], d, tab, edges)

            colours, through = composite((element(d) for d in range(1, depth - 1)), backward)
            for k, value in enumerate(colours + [through]):
                mid[b, k, pl.ds((g - 1) * SUBS, SUBS), :] = value
            return carry

        for h in range(2):
            bin_copies[g, h].wait()
            lax.fori_loop(h * half // LANES, (h + 1) * half // LANES, tile, 0, unroll=4)
    for g in (0, groups - 1):
        for h in range(2):
            bin_copies[g, h].wait()


def outer_kernel(wide, narrow, cells, slopes, zin, zout, xin, xout, picks, mid, tab, back, out):
    depth, cols, rows = picks.shape[1:]
    groups = cols // SUBS
    edges = ends(0, SUBS)
    odd = wide[0] % 2 == 1, narrow[0] % 2 == 1
    for g in range(groups):
        backward = back[g * SUBS : (g + 1) * SUBS, :] == 1
        inside = 0 < g < groups - 1

        def tile(b, carry, g=g, backward=backward, inside=inside):
            start = pl.multiple_of(b * LANES, LANES)
            at = lattice(cells, (xin, xout), (zin, zout), odd, g, start)

            def element(d):
                here = pl.ds(g * SUBS, SUBS), pl.ds(start, LANES)
                return cell(at, lambda f: slopes[f, d, *here], lambda f: picks[f, d, *here], d, tab, edges)

            if inside:
                middle = [mid[b, k, pl.ds((g - 1) * SUBS, SUBS), :] for k in range(4)]
                elements = [element(0), (middle[:3], middle[3]), element(depth - 1)]
            else:
                elements = (element(d) for d in range(depth))
            colours, through = composite(elements, backward)
            for k, value in enumerate(colours):
                out[b, k, pl.ds(g * SUBS, SUBS), :] = value * COLOUR_UNIT
            out[b, 3, pl.ds(g * SUBS, SUBS), :] = 1.0 - through
            return carry

        lax.fori_loop(0, rows // LANES, tile, 0, unroll=8)


VMEM = pl.BlockSpec(memory_space=pltpu.VMEM)
SMEM = pl.BlockSpec(memory_space=pltpu.SMEM)
ANY = pl.BlockSpec(memory_space=pl.ANY)
LIMIT = 24 * 2**20


def load(wide, narrow, fields, colour, opacity, view):
    _, depth, cols, rows = fields.shape
    fields, colour, opacity, view = (pltpu.with_memory_space_constraint(x, pltpu.HBM) for x in (fields, colour, opacity, view))
    return pl.pallas_call(
        load_kernel,
        out_shape=[
            pltpu.VMEM((2, depth, cols, rows), jnp.float32),
            pltpu.VMEM((2, depth, 1, rows), jnp.float32),
            pltpu.VMEM((2, depth, 1, rows), jnp.float32),
            pltpu.VMEM((2, 1, cols, rows), jnp.float32),
            pltpu.VMEM((2, 1, cols, rows), jnp.float32),
            pltpu.VMEM((2, 2, 2, SUBS, LANES), jnp.int32),
            pltpu.VMEM((cols, LANES), jnp.int32),
        ],
        in_specs=[SMEM, SMEM, ANY, ANY, ANY, ANY],
        out_specs=[VMEM] * 7,
        scratch_shapes=[
            pltpu.VMEM(colour.shape, colour.dtype),
            pltpu.VMEM(opacity.shape, opacity.dtype),
            pltpu.SMEM(view.shape, view.dtype),
            pltpu.SemaphoreType.DMA((depth,)),
            pltpu.SemaphoreType.DMA((3,)),
        ],
        compiler_params=pltpu.CompilerParams(vmem_limit_bytes=LIMIT),
        name="load",
    )(wide, narrow, fields, colour, opacity, view)


def march_inner(bins, cells, tab, back):
    _, depth, cols, rows = bins.shape
    return pl.pallas_call(
        inner_kernel,
        out_shape=[
            pltpu.VMEM((2, depth, cols, rows), jnp.int32),
            pltpu.VMEM((2, depth, cols, rows), jnp.float32),
            pltpu.VMEM((rows // LANES, 4, cols - 2 * SUBS, LANES), jnp.float32),
        ],
        in_specs=[ANY] + [VMEM] * 3,
        out_specs=[VMEM] * 3,
        scratch_shapes=[pltpu.SemaphoreType.DMA((cols // SUBS, 2))],
        compiler_params=pltpu.CompilerParams(vmem_limit_bytes=LIMIT),
        cost_estimate=pl.CostEstimate(flops=100 * 2 * depth * cols * rows, bytes_accessed=8 * 2**20, transcendentals=0),
        name="march_inner",
    )(pltpu.with_memory_space_constraint(bins, pltpu.HBM), cells, tab, back)


def march_outer(wide, narrow, cells, slopes, zin, zout, xin, xout, picks, mid, tab, back):
    _, depth, cols, rows = picks.shape
    return pl.pallas_call(
        outer_kernel,
        out_shape=pltpu.VMEM((rows // LANES, 4, cols, LANES), jnp.float32),
        in_specs=[SMEM] * 2 + [VMEM] * 10,
        out_specs=VMEM,
        compiler_params=pltpu.CompilerParams(vmem_limit_bytes=LIMIT),
        name="march_outer",
    )(wide, narrow, cells, slopes, zin, zout, xin, xout, picks, mid, tab, back)


def join_kernel(parts, back, out):
    depth, _, cols, _ = parts.shape
    for group in range(cols // SUBS):
        span = pl.ds(group * SUBS, SUBS)
        elements = (([parts[d, k, span, :] for k in range(3)], 1.0 - parts[d, 3, span, :]) for d in range(depth))
        colour, through = composite(elements, back[span, :] == 1)
        for k in range(3):
            out[k, span, :] = colour[k]
        out[3, span, :] = 1.0 - through


def join(parts, back):
    return pl.pallas_call(
        join_kernel,
        out_shape=pltpu.VMEM(parts.shape[1:], jnp.float32),
        in_specs=[VMEM, VMEM],
        out_specs=VMEM,
        name="join",
    )(pltpu.with_memory_space_constraint(parts, pltpu.VMEM), back)


Z, X, CORES = 8, 4, 2
PIECES = 4


def device(z, x, core):
    return (z % Z * X + x % X) * CORES + core


def everywhere(target):
    places = [(z, x, core) for z in range(Z) for x in range(X) for core in range(CORES)]
    return [(device(*spot), device(*target(*spot))) for spot in places]


def pairs(partner):
    return [list(pair) for pair in everywhere(partner) if pair[0] < pair[1]]


DOUBLINGS = (
    pairs(lambda z, x, core: (z ^ 4, x, core) if core else (z ^ 2, x, core)),
    pairs(lambda z, x, core: (z, x ^ 2, core) if core else (z ^ 4, x, core)),
    pairs(lambda z, x, core: (z, x ^ 1, core) if core else (z ^ 1, x, core)),
)


def beside(place):
    return place + 1 if place % 2 else place - 1


MOVES = (
    everywhere(lambda z, x, core: (z ^ 1, x, core) if core else (z, x ^ 1, core)),
    everywhere(lambda z, x, core: (beside(z), x, core) if core else (z, beside(x), core)),
    everywhere(lambda z, x, core: (z - 2 if z % 2 else z + 2, x, core) if core else (z, x + 2, core)),
)
SWAP = everywhere(lambda z, x, core: (z, x, 1 - core))


def gather(block):
    for groups in DOUBLINGS:
        block = lax.all_gather(block, "wide", axis_index_groups=groups)
    return [block] + [lax.ppermute(block, "wide", move) for move in MOVES]


def place_kernel(swapped, spot, *refs):
    pieces, out, sem = refs[:PIECES], refs[-2], refs[-1]
    wide = spot[0]
    core = (wide + swapped) % CORES
    x, z = wide // CORES % X, wide // (CORES * X)
    copies = []
    for piece in range(PIECES):
        steps = (0, 1 - 2 * (z % 2), 2 * (z % 2) - 1, 2), (0, 1 - 2 * (x % 2), 2 * (x % 2) - 1, 2)
        z_from, x_from = (z + Z + steps[0][piece]) % (Z // 2), (x + X + steps[1][piece]) % X
        for third in range(2):
            for second in range(2):
                for first in range(2):
                    z_now = jnp.where(core == 0, 2 * first + 4 * second + third, 4 * first + z_from)
                    x_now = jnp.where(core == 0, x_from, 2 * second + third)
                    target = out.at[:, z_now, x_now, core]
                    copies.append(pltpu.make_async_copy(pieces[piece].at[third, second, first], target, sem))
    for copy in copies:
        copy.start()
    for copy in copies:
        copy.wait()


def place(pieces, spot, swapped, frame=None):
    channels, cols, rows = pieces[0].shape[3:]
    kept = [] if frame is None else [frame]
    return pl.pallas_call(
        functools.partial(place_kernel, swapped),
        in_specs=[SMEM] + [VMEM] * PIECES + [ANY] * len(kept),
        out_specs=ANY,
        out_shape=jax.ShapeDtypeStruct((channels, Z, X, CORES, cols, rows), jnp.float32),
        scratch_shapes=[pltpu.SemaphoreType.DMA],
        input_output_aliases={1 + PIECES: 0} if kept else {},
        compiler_params=pltpu.CompilerParams(vmem_limit_bytes=2**20),
        cost_estimate=pl.CostEstimate(flops=0, bytes_accessed=4 * 2**20, transcendentals=0),
        name="place",
    )(spot, *(pltpu.with_memory_space_constraint(piece, pltpu.VMEM) for piece in pieces), *kept)


def change(inner, outer, axis):
    count = lax.axis_size(axis)
    route = [(i, beside(i)) for i in range(count) if 0 <= beside(i) < count]
    return lax.ppermute(inner, axis, [(i, i ^ 1) for i in range(count)]), lax.ppermute(outer, axis, route)


def on_device(fields, field_bins, colour_table, opacity_table, view_dir):
    wide, narrow = (lax.axis_index(axis).reshape(1) for axis in ("wide", "narrow"))
    colour = jnp.transpose(colour_table, (1, 0, 2))
    cells, *faces, tab, back = load(wide, narrow, fields, colour, opacity_table, view_dir)
    zin, zout = change(*faces[2:], "narrow")
    xin, xout = change(*faces[:2], "wide")
    picks, slopes, mid = march_inner(field_bins, cells, tab, back)
    partial = march_outer(wide, narrow, cells, slopes, zin, zout, xin, xout, picks, mid, tab, back)
    partial = lax.all_to_all(partial, "narrow", 0, 0)
    own = gather(join(partial, back))
    other = [lax.ppermute(piece, "wide", SWAP) for piece in own]
    frame = place(other, wide, 1, place(own, wide, 0))
    return frame.reshape(frame.shape[0], -1, frame.shape[-1])


def solution(mesh):
    split = P(None, "narrow", "wide", None)
    return jax.shard_map(
        on_device,
        mesh=mesh,
        in_specs=(split, split, P(), P(), P("wide")),
        out_specs=P(None, None, "narrow"),
        check_vma=False,
    )
```

```python
import functools

import jax
import jax.numpy as jnp
from jax import lax
from jax.experimental import pallas as pl
from jax.experimental.pallas import tpu as pltpu
from jax.sharding import PartitionSpec as P

LANES = 128
SUBS = 8
COLOUR_UNIT = 2.0**-12
OPACITY_UNIT = 2.0**-18
FIELD = 1 << 13

LOOKUP = lax.GatherDimensionNumbers(
    offset_dims=(),
    collapsed_slice_dims=(1,),
    start_index_map=(1,),
    operand_batching_dims=(0,),
    start_indices_batching_dims=(0,),
)


def pick(table, lanes):
    return lax.gather(table, lanes[..., None], LOOKUP, (1, 1), mode=lax.GatherScatterMode.PROMISE_IN_BOUNDS)


def store_tables(colour_ref, opacity_ref, tab):
    for f in range(2):
        colour = [(colour_ref[k, f : f + 1, :].astype(jnp.float32) / COLOUR_UNIT).astype(jnp.int32) for k in range(3)]
        opacity = (opacity_ref[f : f + 1, :].astype(jnp.float32) / OPACITY_UNIT).astype(jnp.int32)
        for w, word in enumerate((colour[0] + colour[1] * FIELD, colour[2] + opacity * FIELD)):
            for h in range(2):
                tab[f, w, h] = jnp.broadcast_to(word[:, h * LANES : (h + 1) * LANES], (SUBS, LANES))


def ends(axis, length):
    place = lax.broadcasted_iota(jnp.int32, (SUBS, LANES), axis)
    return place == 0, place == length - 1


def cell(at, slope, bins_of, d, tab, edges):
    first_sub, last_sub = edges
    colour = clear = None
    for f in range(2):
        here = at(f, d, 0)
        dz = at(f, d + 1, 0) - at(f, d - 1, 0)
        after = pltpu.roll(jnp.where(first_sub, at(f, d, SUBS), here), SUBS - 1, 0)
        before = pltpu.roll(jnp.where(last_sub, at(f, d, -SUBS), here), 1, 0)
        dx = after - before
        dy = slope(f)
        total = dz * dz + dx * dx + dy * dy
        shade = 0.3 + (0.35 * jnp.abs(dz)) * lax.rsqrt(0.25 * total + 1.0)
        root = total * lax.rsqrt(jnp.maximum(total, 1e-30))
        gain = 0.25 * OPACITY_UNIT + (0.5 * OPACITY_UNIT) * root
        entry = bins_of(f)
        low = entry & (LANES - 1)
        upper = entry >= LANES
        words = [jnp.where(upper, pick(tab[f, w, 1], low), pick(tab[f, w, 0], low)) for w in range(2)]
        alpha = (words[1] >> 13).astype(jnp.float32) * gain
        lit = alpha * shade
        looked = (words[0] & (FIELD - 1), words[0] >> 13, words[1] & (FIELD - 1))
        terms = [lit * value.astype(jnp.float32) for value in looked]
        colour = terms if colour is None else [a + b for a, b in zip(colour, terms)]
        clear = 1.0 - alpha if clear is None else clear * (1.0 - alpha)
    return colour, clear


def composite(elements, backward):
    colour = through = None
    for part, clear in elements:
        if colour is None:
            colour, through = part, clear
        else:
            keep = jnp.where(backward, clear, 1.0)
            weight = jnp.where(backward, 1.0, through)
            colour = [a * keep + weight * b for a, b in zip(colour, part)]
            through = through * clear
    return colour, through


def lattice(cells, columns, depths, odd, g, start):
    _, depth, cols, _ = cells.shape
    span, here = pl.ds(g * SUBS, SUBS), pl.ds(start, LANES)

    def ghost(faces, is_odd, after, *index):
        inner, outer = (face[index] for face in faces)
        return jnp.where(is_odd != after, inner, outer)

    def at(f, d, dc):
        if d < 0 or d == depth:
            return ghost(depths, odd[1], d == depth, f, 0, span, here)
        if g * SUBS + dc < 0 or g * SUBS + dc == cols:
            face = ghost(columns, odd[0], dc > 0, f, d, slice(None), here)
            return jnp.broadcast_to(face, (SUBS, LANES))
        return cells[f, d, pl.ds(g * SUBS + dc, SUBS), here]

    return at


def load_kernel(
    wide, narrow, fields, colour, opacity, view, cells, xin, xout, zin, zout, tab, back, colour_now, opacity_now, view_now, field_sem, tab_sem
):
    depth, cols, rows = fields.shape[1:]
    small = [
        pltpu.make_async_copy(source, target, tab_sem.at[n])
        for n, (source, target) in enumerate(((colour, colour_now), (opacity, opacity_now), (view, view_now)))
    ]
    for copy in small:
        copy.start()
    sides = (0, depth - 1)
    order = sides + tuple(range(1, depth - 1))
    copies = {}
    for d in order:
        copies[d] = pltpu.make_async_copy(fields.at[:, d], cells.at[:, d], field_sem.at[d])
        copies[d].start()
    for copy in small:
        copy.wait()
    sub = lax.broadcasted_iota(jnp.int32, (SUBS, LANES), 0)
    for g in range(cols // SUBS):
        towards = jnp.zeros((SUBS, LANES), jnp.int32)
        for k in range(SUBS):
            towards = jnp.where(sub == k, view_now[g * SUBS + k], towards)
        back[g * SUBS : (g + 1) * SUBS, :] = towards
    store_tables(colour_now, opacity_now, tab)
    x_odd, z_odd = wide[0] % 2 == 1, narrow[0] % 2 == 1
    for n, d in enumerate(order):
        copies[d].wait()
        for f in range(2):
            low, high = cells[f, d, 0:1, :], cells[f, d, cols - 1 : cols, :]
            xin[f, d] = jnp.where(x_odd, low, high)
            xout[f, d] = jnp.where(x_odd, high, low)
            if n == 1:
                low, high = (cells[f, end] for end in sides)
                zin[f, 0] = jnp.where(z_odd, low, high)
                zout[f, 0] = jnp.where(z_odd, high, low)


def inner_kernel(bins, cells, tab, back, picks, slopes, mid, bin_sem):
    depth, cols, rows = bins.shape[1:]
    groups, half = cols // SUBS, rows // 2
    bin_copies = {}
    inner = range(1, groups - 1)
    for g in (*inner, 0, groups - 1):
        for h in range(2):
            part = pl.ds(g * SUBS, SUBS), pl.ds(h * half, half)
            bin_copies[g, h] = pltpu.make_async_copy(bins.at[:, :, *part], picks.at[:, :, *part], bin_sem.at[g, h])
            bin_copies[g, h].start()
    first_lane, last_lane = ends(1, LANES)
    zero = jnp.zeros((SUBS, LANES), jnp.float32)

    def differ(step, carry):
        d, span = step // groups, pl.ds(pl.multiple_of(step % groups * SUBS, SUBS), SUBS)
        for f in range(2):
            tiles = [zero] + [cells[f, d, span, b * LANES : (b + 1) * LANES] for b in range(rows // LANES)] + [zero]
            for b in range(rows // LANES):
                before, here, after = tiles[b : b + 3]
                after = pltpu.roll(jnp.where(first_lane, after, here), LANES - 1, 1)
                before = pltpu.roll(jnp.where(last_lane, before, here), 1, 1)
                slopes[f, d, span, b * LANES : (b + 1) * LANES] = after - before
        return carry

    lax.fori_loop(0, depth * groups, differ, 0, unroll=4)
    edges = ends(0, SUBS)
    for g in inner:
        backward = back[g * SUBS : (g + 1) * SUBS, :] == 1

        def tile(b, carry, g=g, backward=backward):
            start = pl.multiple_of(b * LANES, LANES)
            at = lattice(cells, None, None, None, g, start)

            def element(d):
                here = pl.ds(g * SUBS, SUBS), pl.ds(start, LANES)
                return cell(at, lambda f: slopes[f, d, *here], lambda f: picks[f, d, *here], d, tab, edges)

            colours, through = composite((element(d) for d in range(1, depth - 1)), backward)
            for k, value in enumerate(colours + [through]):
                mid[b, k, pl.ds((g - 1) * SUBS, SUBS), :] = value
            return carry

        for h in range(2):
            bin_copies[g, h].wait()
            lax.fori_loop(h * half // LANES, (h + 1) * half // LANES, tile, 0, unroll=4)
    for g in (0, groups - 1):
        for h in range(2):
            bin_copies[g, h].wait()


def outer_kernel(wide, narrow, cells, slopes, zin, zout, xin, xout, picks, mid, tab, back, out):
    depth, cols, rows = picks.shape[1:]
    groups = cols // SUBS
    edges = ends(0, SUBS)
    odd = wide[0] % 2 == 1, narrow[0] % 2 == 1
    for g in range(groups):
        backward = back[g * SUBS : (g + 1) * SUBS, :] == 1
        inside = 0 < g < groups - 1

        def tile(b, carry, g=g, backward=backward, inside=inside):
            start = pl.multiple_of(b * LANES, LANES)
            at = lattice(cells, (xin, xout), (zin, zout), odd, g, start)

            def element(d):
                here = pl.ds(g * SUBS, SUBS), pl.ds(start, LANES)
                return cell(at, lambda f: slopes[f, d, *here], lambda f: picks[f, d, *here], d, tab, edges)

            if inside:
                middle = [mid[b, k, pl.ds((g - 1) * SUBS, SUBS), :] for k in range(4)]
                elements = [element(0), (middle[:3], middle[3]), element(depth - 1)]
            else:
                elements = (element(d) for d in range(depth))
            colours, through = composite(elements, backward)
            for k, value in enumerate(colours):
                out[b, k, pl.ds(g * SUBS, SUBS), :] = value * COLOUR_UNIT
            out[b, 3, pl.ds(g * SUBS, SUBS), :] = 1.0 - through
            return carry

        lax.fori_loop(0, rows // LANES, tile, 0, unroll=8)


VMEM = pl.BlockSpec(memory_space=pltpu.VMEM)
SMEM = pl.BlockSpec(memory_space=pltpu.SMEM)
ANY = pl.BlockSpec(memory_space=pl.ANY)
LIMIT = 24 * 2**20


def load(wide, narrow, fields, colour, opacity, view):
    _, depth, cols, rows = fields.shape
    fields, colour, opacity, view = (pltpu.with_memory_space_constraint(x, pltpu.HBM) for x in (fields, colour, opacity, view))
    return pl.pallas_call(
        load_kernel,
        out_shape=[
            pltpu.VMEM((2, depth, cols, rows), jnp.float32),
            pltpu.VMEM((2, depth, 1, rows), jnp.float32),
            pltpu.VMEM((2, depth, 1, rows), jnp.float32),
            pltpu.VMEM((2, 1, cols, rows), jnp.float32),
            pltpu.VMEM((2, 1, cols, rows), jnp.float32),
            pltpu.VMEM((2, 2, 2, SUBS, LANES), jnp.int32),
            pltpu.VMEM((cols, LANES), jnp.int32),
        ],
        in_specs=[SMEM, SMEM, ANY, ANY, ANY, ANY],
        out_specs=[VMEM] * 7,
        scratch_shapes=[
            pltpu.VMEM(colour.shape, colour.dtype),
            pltpu.VMEM(opacity.shape, opacity.dtype),
            pltpu.SMEM(view.shape, view.dtype),
            pltpu.SemaphoreType.DMA((depth,)),
            pltpu.SemaphoreType.DMA((3,)),
        ],
        compiler_params=pltpu.CompilerParams(vmem_limit_bytes=LIMIT),
        name="load",
    )(wide, narrow, fields, colour, opacity, view)


def march_inner(bins, cells, tab, back):
    _, depth, cols, rows = bins.shape
    return pl.pallas_call(
        inner_kernel,
        out_shape=[
            pltpu.VMEM((2, depth, cols, rows), jnp.int32),
            pltpu.VMEM((2, depth, cols, rows), jnp.float32),
            pltpu.VMEM((rows // LANES, 4, cols - 2 * SUBS, LANES), jnp.float32),
        ],
        in_specs=[ANY] + [VMEM] * 3,
        out_specs=[VMEM] * 3,
        scratch_shapes=[pltpu.SemaphoreType.DMA((cols // SUBS, 2))],
        compiler_params=pltpu.CompilerParams(vmem_limit_bytes=LIMIT),
        cost_estimate=pl.CostEstimate(flops=100 * 2 * depth * cols * rows, bytes_accessed=8 * 2**20, transcendentals=0),
        name="march_inner",
    )(pltpu.with_memory_space_constraint(bins, pltpu.HBM), cells, tab, back)


def march_outer(wide, narrow, cells, slopes, zin, zout, xin, xout, picks, mid, tab, back):
    _, depth, cols, rows = picks.shape
    return pl.pallas_call(
        outer_kernel,
        out_shape=pltpu.VMEM((rows // LANES, 4, cols, LANES), jnp.float32),
        in_specs=[SMEM] * 2 + [VMEM] * 10,
        out_specs=VMEM,
        compiler_params=pltpu.CompilerParams(vmem_limit_bytes=LIMIT),
        name="march_outer",
    )(wide, narrow, cells, slopes, zin, zout, xin, xout, picks, mid, tab, back)


def join_kernel(parts, back, out):
    depth, _, cols, _ = parts.shape
    for group in range(cols // SUBS):
        span = pl.ds(group * SUBS, SUBS)
        elements = (([parts[d, k, span, :] for k in range(3)], 1.0 - parts[d, 3, span, :]) for d in range(depth))
        colour, through = composite(elements, back[span, :] == 1)
        for k in range(3):
            out[k, span, :] = colour[k]
        out[3, span, :] = 1.0 - through


def join(parts, back):
    return pl.pallas_call(
        join_kernel,
        out_shape=pltpu.VMEM(parts.shape[1:], jnp.float32),
        in_specs=[VMEM, VMEM],
        out_specs=VMEM,
        name="join",
    )(pltpu.with_memory_space_constraint(parts, pltpu.VMEM), back)


Z, X, CORES = 8, 4, 2


def device(z, x, core):
    return (z % Z * X + x % X) * CORES + core


def everywhere(target):
    places = [(z, x, core) for z in range(Z) for x in range(X) for core in range(CORES)]
    return [(device(*spot), device(*target(*spot))) for spot in places]


def pairs(partner):
    return [list(pair) for pair in everywhere(partner) if pair[0] < pair[1]]


DOUBLINGS = (
    pairs(lambda z, x, core: (z ^ 4, x, core) if core else (z ^ 2, x, core)),
    pairs(lambda z, x, core: (z, x ^ 2, core) if core else (z ^ 4, x, core)),
    pairs(lambda z, x, core: (z, x ^ 1, core) if core else (z ^ 1, x, core)),
)


def beside(place):
    return place + 1 if place % 2 else place - 1


MOVES = (
    everywhere(lambda z, x, core: (z ^ 1, x, core) if core else (z, x ^ 1, core)),
    everywhere(lambda z, x, core: (beside(z), x, core) if core else (z, beside(x), core)),
    everywhere(lambda z, x, core: (z - 2 if z % 2 else z + 2, x, core) if core else (z, x + 2, core)),
)
SWAP = everywhere(lambda z, x, core: (z, x, 1 - core))


def place_kernel(plan, spot, *refs):
    pieces, out, sem = refs[: len(plan)], refs[-2], refs[-1]
    wide = spot[0]
    x, z = wide // CORES % X, wide // (CORES * X)
    copies = []
    for ref, (piece, swapped) in zip(pieces, plan):
        core = (wide + swapped) % CORES
        z_from, x_from = (place + (0, 1 - 2 * (place % 2), 2 * (place % 2) - 1, 2)[piece] for place in (z + Z, x + X))
        z_from, x_from = z_from % (Z // 2), x_from % X
        for third in range(2):
            for second in range(2):
                for first in range(2):
                    z_now = jnp.where(core == 0, 2 * first + 4 * second + third, 4 * first + z_from)
                    x_now = jnp.where(core == 0, x_from, 2 * second + third)
                    target = out.at[:, z_now, x_now, core]
                    copies.append(pltpu.make_async_copy(ref.at[third, second, first], target, sem))
    for copy in copies:
        copy.start()
    for copy in copies:
        copy.wait()


def place(plan, pieces, spot, frame=None):
    channels, cols, rows = pieces[0].shape[3:]
    kept = [] if frame is None else [frame]
    return pl.pallas_call(
        functools.partial(place_kernel, plan),
        in_specs=[SMEM] + [VMEM] * len(pieces) + [ANY] * len(kept),
        out_specs=ANY,
        out_shape=jax.ShapeDtypeStruct((channels, Z, X, CORES, cols, rows), jnp.float32),
        scratch_shapes=[pltpu.SemaphoreType.DMA],
        input_output_aliases={1 + len(pieces): 0} if kept else {},
        compiler_params=pltpu.CompilerParams(vmem_limit_bytes=2**20),
        cost_estimate=pl.CostEstimate(flops=0, bytes_accessed=4 * 2**20, transcendentals=0),
        name="place",
    )(spot, *(pltpu.with_memory_space_constraint(piece, pltpu.VMEM) for piece in pieces), *kept)


def gather(block, wide):
    for groups in DOUBLINGS:
        block = lax.all_gather(block, "wide", axis_index_groups=groups)
    pieces = [block] + [lax.ppermute(block, "wide", move) for move in MOVES]
    swapped = [lax.ppermute(piece, "wide", SWAP) for piece in pieces]
    early, late = (0, 3), (1, 2)
    plan = tuple((piece, 0) for piece in range(4)) + tuple((piece, 1) for piece in early)
    frame = place(plan, pieces + [swapped[piece] for piece in early], wide)
    return place(tuple((piece, 1) for piece in late), [swapped[piece] for piece in late], wide, frame)


def change(inner, outer, axis):
    count = lax.axis_size(axis)
    route = [(i, beside(i)) for i in range(count) if 0 <= beside(i) < count]
    return lax.ppermute(inner, axis, [(i, i ^ 1) for i in range(count)]), lax.ppermute(outer, axis, route)


def on_device(fields, field_bins, colour_table, opacity_table, view_dir):
    wide, narrow = (lax.axis_index(axis).reshape(1) for axis in ("wide", "narrow"))
    colour = jnp.transpose(colour_table, (1, 0, 2))
    cells, *faces, tab, back = load(wide, narrow, fields, colour, opacity_table, view_dir)
    zin, zout = change(*faces[2:], "narrow")
    xin, xout = change(*faces[:2], "wide")
    picks, slopes, mid = march_inner(field_bins, cells, tab, back)
    partial = march_outer(wide, narrow, cells, slopes, zin, zout, xin, xout, picks, mid, tab, back)
    partial = lax.all_to_all(partial, "narrow", 0, 0)
    frame = gather(join(partial, back), wide)
    return frame.reshape(frame.shape[0], -1, frame.shape[-1])


def solution(mesh):
    split = P(None, "narrow", "wide", None)
    return jax.shard_map(
        on_device,
        mesh=mesh,
        in_specs=(split, split, P(), P(), P("wide")),
        out_specs=P(None, None, "narrow"),
        check_vma=False,
    )
```
